512 devices in a mesh: pool: 2 (over core), grp: 32 (over x, z), tp: 8 (over y).
Axes of the slice: x: 4, y: 8, z: 8, core: 2. Of those that a mesh axis runs over, the one named last changes fastest.
Arguments:
- queries: bfloat16 [1024, 8192], P('grp', ('pool', 'tp')), may hold values from -6 to 6
- keys: bfloat16 [1024, 32, 256], P('grp'), may hold values from -6 to 6
- values: bfloat16 [1024, 32, 256], P('grp'), may hold values from -6 to 6
- lengths: int32 [1024], P('grp'), may hold values from 2 to 32
- out_weight: bfloat16 [8192, 7168], P(('pool', 'tp'), 'grp'), may hold values from -0.0625 to 0.0625
- residual: bfloat16 [1024, 7168], P(('pool', 'tp'), 'grp'), may hold values from -6 to 6
- norm_gain: float32 [7168], replicated, may hold values from 0.25 to 1.75
- routes: int32 [1024, 3], replicated, may hold values from 0 to 15, all different within a row; in each aligned block of 64 rows (0 to 63, 64 to 127, ...) at most 24 rows name the same one
- route_weight: float32 [1024, 3], replicated, may hold values from 0.2 to 1
- up_weight: bfloat16 [16, 7168, 4096], P(('pool', 'tp'), None, 'grp'), may hold values from -0.0625 to 0.0625
- down_weight: bfloat16 [16, 7168, 4096], P(('pool', 'tp'), 'grp'), may hold values from -0.09375 to 0.09375
Outputs:
- expert_sum: bfloat16 [1024, 7168], P(('pool', 'tp'), 'grp')
The draws below stay inside these ranges and needn't reach their ends.
Inputs may be any that keep to these rules, and one draw needn't show every extreme that they name: `routes`: in the rows of one block, no expert is named more than 24 times, a bound that some block reaches.
All inputs are finite; a program needn't handle non-finite values.
Results may differ from the reference program's by a relative error of at most 0.029.
Values may be sent and summed in bfloat16 or wider, within the bound.
No kernel may reach another device: no remote copies, remote signals or barrier semaphores. Data moves between devices by JAX's collectives and lax.ppermute only.
A program may use at most 64 MiB of HBM per device.

```python
import math
import jax
import jax.numpy as jnp
import numpy as np
from jax import lax

D = 7168
HD = 256
HEADS = 32
FFW = 4096
TOP = 3
CTX = 32
BLOCK_ROWS = 64
EXPERTS = 16
SLOT_CAP = 24
ROWS = 1024


def draw_keys(key, part):
    key = jax.random.fold_in(key, 7)
    base = jnp.clip(jax.random.normal(key, (ROWS, CTX, HD), jnp.float32), -6.0, 6.0)
    return base.astype(jnp.bfloat16)


def draw_queries(key, part):
    key = jax.random.fold_in(key, 5)
    base = jnp.clip(jax.random.normal(key, (ROWS, HEADS, HD), jnp.float32), -6.0, 6.0)
    return base.reshape(ROWS, HEADS * HD).astype(jnp.bfloat16)


def plant(array, rng, low, largest):
    place = [jax.random.randint(jax.random.fold_in(rng, axis), (), 0, length) for axis, length in enumerate(array.shape)]
    widest = array.shape.index(max(array.shape))
    neighbour = place[:widest] + [(place[widest] + 1) % array.shape[widest]] + place[widest + 1:]
    return array.at[tuple(place)].set(low).at[tuple(neighbour)].set(largest)


def level_of(own_key, shape, cuts, low, largest):
    gain = 1.0
    for dim, blocks in cuts:
        heights = jax.random.uniform(jax.random.fold_in(jax.random.fold_in(own_key, 6), dim), (blocks,), jnp.float32, low / len(cuts), largest / len(cuts))
        gain = gain * jnp.repeat(jnp.exp(heights), shape[dim] // blocks).reshape((-1,) + (1,) * (len(shape) - 1 - dim))
    return gain


def assign_block(rng, own, number, rows, amount, top, limit, lean):
    ranking = jax.random.permutation(rng, amount)
    crowded, common = shares(amount, rows * top, limit, lean, True), shares(amount, rows * top, limit, lean, False)
    places = jnp.arange(amount)

    def named(sizes, offset_by):
        used = int((sizes > 0).sum())
        fixed = max(1, used // 4)
        shifted = fixed + (places - fixed + offset_by * (used - fixed)) % max(1, amount - fixed)
        return jnp.zeros((amount,), jnp.int32).at[ranking[jnp.where(places < fixed, places, shifted)]].set(jnp.asarray(sizes, jnp.int32))

    sizes = jnp.where(number % 4 == 0, named(crowded, number // 4), named(common, number - number // 4 - 1))
    mixed = jax.random.permutation(jax.random.fold_in(own, 3), amount)
    source_of, receiver = mixed[0:amount // 2 * 2:2], mixed[1:amount // 2 * 2:2]
    slack = jnp.minimum(sizes[source_of] - 1, limit - sizes[receiver]) // 2
    slack = jnp.where((source_of == ranking[0]) | (receiver == ranking[0]) | (sizes[receiver] == 0), 0, jnp.maximum(slack, 0))
    shifted = jax.random.randint(jax.random.fold_in(own, 4), (amount // 2,), 0, 1 << 20) % (slack + 1)
    sizes = sizes.at[source_of].add(-shifted).at[receiver].add(shifted)
    members = jnp.searchsorted(jnp.cumsum(sizes), jnp.arange(rows * top), side="right").astype(jnp.int32)
    grid = members.reshape(top, rows).T
    grid = grid[jax.random.permutation(jax.random.fold_in(own, 1), rows)]
    offset_by = jax.random.randint(jax.random.fold_in(own, 2), (rows, 1), 0, top)
    return jnp.take_along_axis(grid, (jnp.arange(top)[None, :] + offset_by) % top, axis=1)


def shares(amount, total, most, slope, full):
    portions = [(1 << 20) // math.isqrt(standing ** slope) + 1 for standing in range(1, amount + 1)]
    largest = most if full else min(most, max(-(-total // amount), total * portions[0] // sum(portions)))
    least = 1 if total - largest >= amount - 1 else 0
    given, spare = [largest] + [least] * (amount - 1), total - largest - least * (amount - 1)
    while spare > 0:
        candidates = [i for i in range(1, amount) if given[i] < largest] or [i for i in range(1, amount) if given[i] < most]
        whole, left = sum([portions[i] for i in candidates]), spare
        for i in candidates:
            addition = min(most - given[i], max(1, left * portions[i] // whole), spare)
            given[i] = given[i] + addition
            spare = spare - addition
    return np.array(given)


def bell_draw(own_key, extent, deviation, limit, pieces=(), kind=jnp.bfloat16):
    array = jax.random.normal(own_key, extent, jnp.float32) * deviation
    if len(pieces) > 0:
        array = level_of(own_key, extent, pieces, -0.22, 0.18) * array
    return jnp.clip(array, min=-limit, max=limit).astype(kind)


def setup_inputs(seed: int = 0) -> dict:
    streams_of = jax.random.split(jax.random.key(seed), 12)
    queries = draw_queries(jax.random.fold_in(streams_of[11], 71), 0)
    keys = draw_keys(jax.random.fold_in(streams_of[11], 71), 0)
    values = bell_draw(streams_of[2], (ROWS, CTX, HD), 1.0, 6.0, ((0, 32),))
    lengths = plant(jax.random.randint(streams_of[3], (ROWS,), 2, CTX + 1), jax.random.fold_in(streams_of[3], 1), 2, CTX).astype(jnp.int32)
    out_weight = bell_draw(streams_of[4], (HEADS * HD, D), (HEADS * HD) ** -0.5, 0.0625, ((0, 16), (1, 32)))
    residual = bell_draw(streams_of[5], (ROWS, D), 1.0, 6.0, ((0, 16), (1, 32)))
    norm_gain = jnp.clip(1.0 + 0.15 * jax.random.normal(streams_of[6], (D,), jnp.float32), 0.25, 1.75)
    routes_keys = jax.random.split(jax.random.fold_in(streams_of[7], 1), ROWS // BLOCK_ROWS)
    routes_turns = jax.random.permutation(jax.random.fold_in(streams_of[7], 3), ROWS // BLOCK_ROWS)
    routes = jax.vmap(lambda own, number: assign_block(jax.random.fold_in(streams_of[7], 2), own, number, BLOCK_ROWS, EXPERTS, TOP, SLOT_CAP, 2))(routes_keys, routes_turns).reshape((ROWS, TOP))
    route_weight = jnp.clip(jax.random.uniform(streams_of[8], (ROWS, TOP), jnp.float32, 0.2, 1.0), 0.2, 1.0)
    up_weight = bell_draw(streams_of[9], (EXPERTS, D, FFW), D ** -0.5, 0.0625, ((0, 16), (2, 32)))
    down_weight = bell_draw(streams_of[10], (EXPERTS, D, FFW), FFW ** -0.5, 0.09375, ((0, 16), (1, 32)))
    return {"queries": queries, "keys": keys, "values": values, "lengths": lengths, "out_weight": out_weight, "residual": residual, "norm_gain": norm_gain, "routes": routes, "route_weight": route_weight, "up_weight": up_weight, "down_weight": down_weight}


def attend(queries, keys, values, lengths):
    query_heads = queries.reshape(ROWS, HEADS, HD).astype(jnp.float32)
    scores = jnp.einsum('rhd,rjd->rhj', query_heads, keys.astype(jnp.float32)) * HD ** (-0.5)
    valid = jnp.arange(CTX, dtype=jnp.int32)[None, None, :] < lengths[:, None, None]
    scores = jnp.where(valid, scores, -1e+30)
    highest = lax.optimization_barrier(jnp.max(scores, axis=-1, keepdims=True))
    weights = jnp.exp(scores - highest)
    probs = (weights / lax.optimization_barrier(jnp.sum(weights, axis=-1, keepdims=True))).astype(jnp.bfloat16)
    attn = jnp.einsum('rhj,rjd->rhd', probs.astype(jnp.float32), values.astype(jnp.float32))
    return attn.astype(jnp.bfloat16).reshape(ROWS, HEADS * HD)

def reference(queries, keys, values, lengths, out_weight, residual, norm_gain, routes, route_weight, up_weight, down_weight):
    attn = attend(queries, keys, values, lengths)
    slice_width = HEADS * HD // EXPERTS
    total = jnp.zeros((ROWS, D), jnp.float32)
    for slice_index in range(EXPERTS):
        lower = slice_index * slice_width
        part = jnp.dot(attn[:, lower:lower + slice_width], out_weight[lower:lower + slice_width], preferred_element_type=jnp.float32)
        first = slice_index * BLOCK_ROWS
        part = part.at[first:first + BLOCK_ROWS].add(residual[first:first + BLOCK_ROWS].astype(jnp.float32))
        rounded = lax.optimization_barrier(part.astype(jnp.bfloat16))
        total = total + rounded.astype(jnp.float32)
    hidden = total.astype(jnp.bfloat16)
    hidden_f = hidden.astype(jnp.float32)
    scale = lax.rsqrt(lax.optimization_barrier(jnp.mean(hidden_f * hidden_f, axis=1)) + 1e-06)
    normed = (hidden_f * norm_gain[None, :]).astype(jnp.bfloat16)
    flat = routes.reshape(-1).astype(jnp.int32)
    pair_count = ROWS * TOP
    sort_keys = flat * pair_count + jnp.arange(pair_count, dtype=jnp.int32)
    order = jnp.argsort(sort_keys, stable=True).astype(jnp.int32)
    counts = lax.optimization_barrier(jnp.sum((flat[:, None] == jnp.arange(EXPERTS, dtype=jnp.int32)[None, :]).astype(jnp.int32), axis=0))
    offsets = (jnp.cumsum(counts) - counts).astype(jnp.int32)
    expert_cap = EXPERTS * SLOT_CAP
    padded = jnp.concatenate([order, jnp.zeros((expert_cap,), jnp.int32)])

    def one_expert(expert, outputs):
        start = lax.dynamic_index_in_dim(offsets, expert, 0, keepdims=False)
        taken = lax.dynamic_slice(padded, (start,), (expert_cap,))
        live = jnp.arange(expert_cap, dtype=jnp.int32) < lax.dynamic_index_in_dim(counts, expert, 0, keepdims=False)
        chosen = taken // TOP
        pre = jnp.dot(normed[chosen], lax.dynamic_index_in_dim(up_weight, expert, 0, keepdims=False), preferred_element_type=jnp.float32)
        act = jax.nn.silu(pre * scale[chosen][:, None]).astype(jnp.bfloat16)
        down = lax.dynamic_index_in_dim(down_weight, expert, 0, keepdims=False)
        result = lax.dot_general(act, down, (((1,), (1,)), ((), ())), preferred_element_type=jnp.float32).astype(jnp.bfloat16)
        target = jnp.where(live, taken, pair_count).astype(jnp.int32)
        return outputs.at[target].set(result, mode='drop')
    outputs = lax.fori_loop(0, EXPERTS, one_expert, jnp.zeros((pair_count, D), jnp.bfloat16))
    per_route = outputs.reshape(ROWS, TOP, D).astype(jnp.float32)
    return lax.optimization_barrier(jnp.sum(route_weight[:, :, None] * per_route, axis=1)).astype(jnp.bfloat16)
```

```python
import jax
import jax.numpy as jnp
from jax import lax
from jax.sharding import PartitionSpec as P

BF16 = jnp.bfloat16
F32 = jnp.float32
NX, NZ, PAIR = 4, 4, 2
GATHER = [[x * 8 + z * 2 + m for z in range(NZ)] for x in range(NX) for m in range(PAIR)]
REDUCE = [[x * 8 + z * 2 + m for x in range(NX) for m in range(PAIR)] for z in range(NZ)]


def spread(value, count, axis, groups=None):
    sent = jnp.broadcast_to(value[None], (count,) + value.shape)
    return lax.all_to_all(sent, axis, 0, 0, tiled=True, axis_index_groups=groups)


def exchange(value, axis, groups=None):
    return lax.all_to_all(value, axis, 0, 0, tiled=True, axis_index_groups=groups)


def attend(queries, keys, values, lengths):
    group_rows, ctx_len, head_size = keys.shape
    query_heads = queries.reshape(group_rows, -1, head_size)
    scores = jnp.einsum("rhd,rjd->rhj", query_heads, keys, preferred_element_type=F32)
    scores = scores * head_size ** (-0.5)
    valid = jnp.arange(ctx_len, dtype=jnp.int32)[None, None, :] < lengths[:, None, None]
    scores = jnp.where(valid, scores, -1e30)
    highest = jnp.max(scores, axis=-1, keepdims=True)
    weights = jnp.exp(scores - highest)
    probs = (weights / jnp.sum(weights, axis=-1, keepdims=True)).astype(BF16)
    attn = jnp.einsum("rhj,rjd->rhd", probs, values, preferred_element_type=F32)
    return attn.astype(BF16).reshape(queries.shape)


def shards(
    queries,
    keys,
    values,
    lengths,
    out_weight,
    residual,
    norm_gain,
    routes,
    route_weight,
    up_weight,
    down_weight,
):
    experts = lax.axis_size(("pool", "tp"))
    groups = lax.axis_size("grp")
    block_index = lax.axis_index(("pool", "tp"))
    pool_index = lax.axis_index("pool")
    group_index = lax.axis_index("grp")
    x_index, member = group_index // (NZ * PAIR), group_index % PAIR
    rows, columns = residual.shape
    top_count = routes.shape[1]
    slot_cap = min(rows, rows * top_count * 2 // experts)
    slots = experts * slot_cap
    width = norm_gain.shape[0]
    units = up_weight.shape[2]
    parts = NX * PAIR

    own_routes = lax.dynamic_slice_in_dim(routes, block_index * rows, rows, 0)
    own_weight = lax.dynamic_slice_in_dim(route_weight, block_index * rows, rows, 0)
    named = own_routes.T[:, None, :] == jnp.arange(experts, dtype=jnp.int32)[None, :, None]
    weight_of = jnp.sum(jnp.where(named, own_weight.T[:, None, :], 0.0), axis=0)
    named = jnp.any(named, axis=0)
    earlier = jnp.arange(rows)[:, None] < jnp.arange(rows)[None, :]
    place = jnp.dot(named.astype(BF16), earlier.astype(BF16), preferred_element_type=F32)
    here = place.astype(jnp.int32)[:, None, :] == jnp.arange(slot_cap, dtype=jnp.int32)[None, :, None]
    here = jnp.logical_and(here, named[:, None, :])
    select = here.astype(BF16).reshape(slots, rows)
    combine = jnp.where(here, weight_of[:, None, :], 0.0).reshape(slots, rows)

    attn = attend(queries, keys, values, lengths)
    attn = spread(attn, groups, "grp").reshape(groups * attn.shape[0], attn.shape[1])

    up_parts = up_weight[0].reshape(NX, NZ, PAIR, columns, units).transpose(0, 2, 1, 3, 4)
    down_parts = down_weight[0].reshape(columns, NX, NZ, PAIR, units).transpose(1, 3, 2, 0, 4)
    both = jnp.concatenate(
        [up_parts.reshape(parts, NZ * columns, units), down_parts.reshape(parts, NZ * columns, units)],
        axis=1,
    )
    attn, both = lax.optimization_barrier((attn, both))
    both = exchange(both, "grp", REDUCE)
    up_own = both[:, : NZ * columns].transpose(1, 0, 2).reshape(NZ * columns, parts * units)
    down_own = both[:, NZ * columns :].reshape(parts, NZ, columns, units).transpose(0, 2, 1, 3)
    down_own = down_own.reshape(parts * columns, NZ * units)

    projected = jnp.dot(attn, out_weight, preferred_element_type=F32).astype(BF16)
    projected = projected.reshape(2, experts // 2 * rows, columns)
    kept = lax.dynamic_index_in_dim(projected, pool_index, 0, keepdims=False)
    sent = lax.dynamic_index_in_dim(projected, 1 - pool_index, 0, keepdims=False)
    got = lax.ppermute(sent, "pool", [(0, 1), (1, 0)])
    pair_sum = (kept.astype(F32) + got.astype(F32)).astype(BF16).reshape(experts // 2, rows, columns)
    hidden = jnp.sum(exchange(pair_sum, "tp").astype(F32), axis=0) + residual.astype(F32)
    hidden = hidden.astype(BF16)

    slot_rows = jnp.dot(select, hidden, preferred_element_type=F32).astype(BF16)
    slot_rows = exchange(slot_rows.reshape(experts, slot_cap, columns), ("pool", "tp"))
    slot_rows = spread(slot_rows.reshape(slots, columns), NZ, "grp", GATHER).astype(F32)
    gain = norm_gain.reshape(NX, NZ, PAIR, columns)
    gain = lax.dynamic_index_in_dim(gain, x_index, 0, keepdims=False)
    gain = lax.dynamic_index_in_dim(gain, member, 1, keepdims=False)
    normed = (slot_rows * gain[:, None, :]).astype(BF16)
    normed = normed.transpose(1, 0, 2).reshape(slots, NZ * columns)
    squares = jnp.sum(slot_rows * slot_rows, axis=(0, 2)).reshape(slots // units, units)
    high = lax.reduce_precision(squares, 8, 7)
    low = squares - high
    pad = jnp.zeros((16 - 2 * (slots // units), units), F32)
    tail = jnp.concatenate([high, low, pad], axis=0).astype(BF16)
    partial_up = jnp.dot(normed, up_own, preferred_element_type=F32).astype(BF16)
    partial_up = partial_up.reshape(slots, parts, units).transpose(1, 0, 2)
    partial_up = jnp.concatenate(
        [partial_up, jnp.broadcast_to(tail[None], (parts,) + tail.shape)], axis=1
    )
    total_up = jnp.sum(exchange(partial_up, "grp", REDUCE).astype(F32), axis=0)
    count = slots // units
    squares = (total_up[slots : slots + count] + total_up[slots + count : slots + 2 * count]).reshape(slots, 1)
    scale = lax.rsqrt(squares / width + 1e-06)
    act = jax.nn.silu(total_up[:slots] * scale).astype(BF16)

    act = spread(act, NZ, "grp", GATHER).transpose(1, 0, 2).reshape(slots, NZ * units)
    partial_out = lax.dot_general(
        down_own, act, (((1,), (1,)), ((), ())), preferred_element_type=F32
    ).astype(BF16)
    partial_out = exchange(partial_out.reshape(parts, columns, slots), "grp", REDUCE)
    expert_out = jnp.sum(partial_out.astype(F32), axis=0).astype(BF16).T
    returned = exchange(expert_out.reshape(experts, slot_cap, columns), ("pool", "tp"))
    returned = returned.reshape(slots, columns)
    high = lax.reduce_precision(combine, 8, 7)
    dims = (((0,), (0,)), ((), ()))
    result = lax.dot_general(high.astype(BF16), returned, dims, preferred_element_type=F32)
    result += lax.dot_general((combine - high).astype(BF16), returned, dims, preferred_element_type=F32)
    return result.astype(BF16)


def solution(mesh):
    placed = (
        P("grp", ("pool", "tp")),
        P("grp", None, None),
        P("grp", None, None),
        P("grp"),
        P(("pool", "tp"), "grp"),
        P(("pool", "tp"), "grp"),
        P(),
        P(),
        P(),
        P(("pool", "tp"), None, "grp"),
        P(("pool", "tp"), "grp", None),
    )
    return jax.shard_map(
        shards, mesh=mesh, in_specs=placed, out_specs=P(("pool", "tp"), "grp"), check_vma=False
    )
```

```python
import jax
import jax.numpy as jnp
from jax import lax
from jax.sharding import PartitionSpec as P

BF16 = jnp.bfloat16
F32 = jnp.float32
NX, NZ, PAIR = 4, 4, 2
GATHER = [[x * 8 + z * 2 + m for z in range(NZ)] for x in range(NX) for m in range(PAIR)]
REDUCE = [[x * 8 + z * 2 + m for x in range(NX) for m in range(PAIR)] for z in range(NZ)]


def moves(by_x, by_member):
    return [
        (x * 8 + z * 2 + m, (x + by_x) % NX * 8 + z * 2 + (m + by_member) % PAIR)
        for x in range(NX)
        for z in range(NZ)
        for m in range(PAIR)
    ]


def spread(value, count, axis, groups=None):
    sent = jnp.broadcast_to(value[None], (count,) + value.shape)
    return lax.all_to_all(sent, axis, 0, 0, tiled=True, axis_index_groups=groups)


def exchange(value, axis, groups=None):
    return lax.all_to_all(value, axis, 0, 0, tiled=True, axis_index_groups=groups)


def attend(queries, keys, values, lengths):
    group_rows, ctx_len, head_size = keys.shape
    query_heads = queries.reshape(group_rows, -1, head_size)
    scores = jnp.einsum("rhd,rjd->rhj", query_heads, keys, preferred_element_type=F32)
    scores = scores * head_size ** (-0.5)
    valid = jnp.arange(ctx_len, dtype=jnp.int32)[None, None, :] < lengths[:, None, None]
    scores = jnp.where(valid, scores, -1e30)
    highest = jnp.max(scores, axis=-1, keepdims=True)
    weights = jnp.exp(scores - highest)
    probs = (weights / jnp.sum(weights, axis=-1, keepdims=True)).astype(BF16)
    attn = jnp.einsum("rhj,rjd->rhd", probs, values, preferred_element_type=F32)
    return attn.astype(BF16).reshape(queries.shape)


def shards(
    queries,
    keys,
    values,
    lengths,
    out_weight,
    residual,
    norm_gain,
    routes,
    route_weight,
    up_weight,
    down_weight,
):
    experts = lax.axis_size(("pool", "tp"))
    block_index = lax.axis_index(("pool", "tp"))
    pool_index = lax.axis_index("pool")
    group_index = lax.axis_index("grp")
    x_index, member = group_index // (NZ * PAIR), group_index % PAIR
    rows, columns = residual.shape
    top_count = routes.shape[1]
    slot_cap = min(rows, rows * top_count * 2 // experts)
    slots = experts * slot_cap
    width = norm_gain.shape[0]
    units = up_weight.shape[2]
    parts = NX * PAIR

    own_routes = lax.dynamic_slice_in_dim(routes, block_index * rows, rows, 0)
    own_weight = lax.dynamic_slice_in_dim(route_weight, block_index * rows, rows, 0)
    named = own_routes.T[:, None, :] == jnp.arange(experts, dtype=jnp.int32)[None, :, None]
    weight_of = jnp.sum(jnp.where(named, own_weight.T[:, None, :], 0.0), axis=0)
    named = jnp.any(named, axis=0)
    earlier = jnp.arange(rows)[:, None] < jnp.arange(rows)[None, :]
    place = jnp.dot(named.astype(BF16), earlier.astype(BF16), preferred_element_type=F32)
    here = place.astype(jnp.int32)[:, None, :] == jnp.arange(slot_cap, dtype=jnp.int32)[None, :, None]
    here = jnp.logical_and(here, named[:, None, :])
    select = here.astype(BF16).reshape(slots, rows)
    combine = jnp.where(here, weight_of[:, None, :], 0.0).reshape(slots, rows)

    attn = attend(queries, keys, values, lengths)
    attn = spread(attn, NZ, "grp", GATHER)
    attn = spread(attn.reshape(-1, attn.shape[2]), parts, "grp", REDUCE)
    attn = attn.reshape(NX, PAIR, NZ, -1, attn.shape[2]).transpose(0, 2, 1, 3, 4)
    attn = attn.reshape(experts * rows, attn.shape[4])

    up_parts = up_weight[0].reshape(NX, NZ, PAIR, columns, units)
    down_parts = down_weight[0].reshape(columns, NX, NZ, PAIR, units).transpose(1, 2, 3, 0, 4)
    held = []
    for step in range(NX):
        wanted = (x_index + step) % NX
        block = jnp.stack(
            [lax.dynamic_index_in_dim(w, wanted, 0, keepdims=False) for w in (up_parts, down_parts)]
        )
        held.append(lax.ppermute(block, "grp", moves(step, 0)) if step else block)
    held = jnp.stack([lax.dynamic_index_in_dim(jnp.stack(held), (x_index - x) % NX, 0, False) for x in range(NX)])
    kept = lax.dynamic_index_in_dim(held, member, 3, keepdims=False)
    sent = lax.dynamic_index_in_dim(held, 1 - member, 3, keepdims=False)
    got = lax.ppermute(sent, "grp", moves(0, 1))
    first, second = jnp.where(member == 0, kept, got), jnp.where(member == 0, got, kept)
    both = jnp.stack([first, second], axis=1)
    up_own = both[:, :, 0].reshape(parts, NZ * columns, units).transpose(1, 0, 2)
    up_own = up_own.reshape(NZ * columns, parts * units)
    down_own = both[:, :, 1].reshape(parts, NZ, columns, units).transpose(0, 2, 1, 3)
    down_own = down_own.reshape(parts * columns, NZ * units)

    projected = jnp.dot(attn, out_weight, preferred_element_type=F32).astype(BF16)
    projected = projected.reshape(2, experts // 2 * rows, columns)
    kept = lax.dynamic_index_in_dim(projected, pool_index, 0, keepdims=False)
    sent = lax.dynamic_index_in_dim(projected, 1 - pool_index, 0, keepdims=False)
    got = lax.ppermute(sent, "pool", [(0, 1), (1, 0)])
    pair_sum = (kept.astype(F32) + got.astype(F32)).astype(BF16).reshape(experts // 2, rows, columns)
    hidden = jnp.sum(exchange(pair_sum, "tp").astype(F32), axis=0) + residual.astype(F32)
    hidden = hidden.astype(BF16)

    slot_rows = jnp.dot(select, hidden, preferred_element_type=F32).astype(BF16)
    slot_rows = exchange(slot_rows.reshape(experts, slot_cap, columns), ("pool", "tp"))
    slot_rows = spread(slot_rows.reshape(slots, columns), NZ, "grp", GATHER).astype(F32)
    gain = norm_gain.reshape(NX, NZ, PAIR, columns)
    gain = lax.dynamic_index_in_dim(gain, x_index, 0, keepdims=False)
    gain = lax.dynamic_index_in_dim(gain, member, 1, keepdims=False)
    normed = (slot_rows * gain[:, None, :]).astype(BF16)
    normed = normed.transpose(1, 0, 2).reshape(slots, NZ * columns)
    squares = jnp.sum(slot_rows * slot_rows, axis=(0, 2)).reshape(slots // units, units)
    high = lax.reduce_precision(squares, 8, 7)
    low = squares - high
    pad = jnp.zeros((16 - 2 * (slots // units), units), F32)
    tail = jnp.concatenate([high, low, pad], axis=0).astype(BF16)
    partial_up = jnp.dot(normed, up_own, preferred_element_type=F32).astype(BF16)
    partial_up = partial_up.reshape(slots, parts, units).transpose(1, 0, 2)
    partial_up = jnp.concatenate(
        [partial_up, jnp.broadcast_to(tail[None], (parts,) + tail.shape)], axis=1
    )
    total_up = jnp.sum(exchange(partial_up, "grp", REDUCE).astype(F32), axis=0)
    count = slots // units
    squares = (total_up[slots : slots + count] + total_up[slots + count : slots + 2 * count]).reshape(slots, 1)
    scale = lax.rsqrt(squares / width + 1e-06)
    act = jax.nn.silu(total_up[:slots] * scale).astype(BF16)

    act = spread(act, NZ, "grp", GATHER).transpose(1, 0, 2).reshape(slots, NZ * units)
    partial_out = lax.dot_general(
        down_own, act, (((1,), (1,)), ((), ())), preferred_element_type=F32
    ).astype(BF16)
    partial_out = exchange(partial_out.reshape(parts, columns, slots), "grp", REDUCE)
    expert_out = jnp.sum(partial_out.astype(F32), axis=0).astype(BF16).T
    returned = exchange(expert_out.reshape(experts, slot_cap, columns), ("pool", "tp"))
    returned = returned.reshape(slots, columns)
    high = lax.reduce_precision(combine, 8, 7)
    dims = (((0,), (0,)), ((), ()))
    result = lax.dot_general(high.astype(BF16), returned, dims, preferred_element_type=F32)
    result += lax.dot_general((combine - high).astype(BF16), returned, dims, preferred_element_type=F32)
    return result.astype(BF16)


def solution(mesh):
    placed = (
        P("grp", ("pool", "tp")),
        P("grp", None, None),
        P("grp", None, None),
        P("grp"),
        P(("pool", "tp"), "grp"),
        P(("pool", "tp"), "grp"),
        P(),
        P(),
        P(),
        P(("pool", "tp"), None, "grp"),
        P(("pool", "tp"), "grp", None),
    )
    return jax.shard_map(
        shards, mesh=mesh, in_specs=placed, out_specs=P(("pool", "tp"), "grp"), check_vma=False
    )
```

```python
import jax
import jax.numpy as jnp
from jax import lax
from jax.experimental import pallas as pl
from jax.experimental.pallas import tpu as pltpu
from jax.sharding import PartitionSpec as P

BF16 = jnp.bfloat16
F32 = jnp.float32
NX, NZ, PAIR = 4, 4, 2
GATHER = [[x * 8 + z * 2 + m for z in range(NZ)] for x in range(NX) for m in range(PAIR)]
LINE = [[x * 8 + z for z in range(8)] for x in range(NX)]
CROSS = [[x * 8 + z for x in range(NX)] for z in range(8)]
REDUCE = [[x * 8 + z * 2 + m for x in range(NX) for m in range(PAIR)] for z in range(NZ)]


def moves(by_x, by_member):
    return [
        (x * 8 + z * 2 + m, (x + by_x) % NX * 8 + z * 2 + (m + by_member) % PAIR)
        for x in range(NX)
        for z in range(NZ)
        for m in range(PAIR)
    ]


def spread(value, count, axis, groups=None):
    sent = jnp.broadcast_to(value[None], (count,) + value.shape)
    return lax.all_to_all(sent, axis, 0, 0, tiled=True, axis_index_groups=groups)


def exchange(value, axis, groups=None):
    return lax.all_to_all(value, axis, 0, 0, tiled=True, axis_index_groups=groups)


def up_kernel(place, rows, gain, block0, block1, block2, block3, got, out):
    x_index, member = place[0], place[1]
    slots, units = rows.shape[1], out.shape[2]
    normed, squares = [], 0.0
    ones = jnp.ones((16, rows.shape[2]), BF16)
    dims = (((1,), (1,)), ((), ()))
    for z in range(NZ):
        value = rows[z].astype(F32)
        normed.append((value * gain[z][None, :]).astype(BF16))
        square = value * value
        high = square.astype(BF16)
        low = (square - high.astype(F32)).astype(BF16)
        squares += lax.dot_general(ones, high, dims, preferred_element_type=F32)
        squares += lax.dot_general(ones, low, dims, preferred_element_type=F32)
    row = lax.broadcasted_iota(jnp.int32, (16, units), 0)
    count = slots // units
    tail = jnp.zeros((16, units), F32)
    for i in range(count):
        part = squares[:, i * units : (i + 1) * units]
        high = part.astype(BF16).astype(F32)
        tail = jnp.where(row == i, high, tail)
        tail = jnp.where(row == count + i, part - high, tail)
    tail = tail.astype(BF16)
    for step, block in enumerate((block0, block1, block2, block3)):
        total = 0.0
        for z in range(NZ):
            both = jnp.concatenate([block[z, member], got[step, z]], axis=1)
            total += jnp.dot(normed[z], both, preferred_element_type=F32)
        total = total.astype(BF16)
        first = lax.rem(x_index + NX - step, NX) * PAIR
        for target, part in ((first + member, total[:, :units]), (first + 1 - member, total[:, units:])):
            out[target, :slots] = part
            out[target, slots:] = tail


def up_product(place, rows, gain, blocks, got):
    slots, columns = rows.shape[1:]
    units = got.shape[3]
    vmem = pl.BlockSpec(memory_space=pltpu.VMEM)
    return pl.pallas_call(
        up_kernel,
        out_shape=jax.ShapeDtypeStruct((NX * PAIR, slots + 16, units), BF16),
        in_specs=[pl.BlockSpec(memory_space=pltpu.SMEM)] + [vmem] * 7,
        out_specs=vmem,
        compiler_params=pltpu.CompilerParams(vmem_limit_bytes=40 * 2**20),
        cost_estimate=pl.CostEstimate(
            flops=2 * slots * columns * NZ * NX * PAIR * units, bytes_accessed=6 * 2**20, transcendentals=0
        ),
    )(place, rows, gain, *blocks, got)


def down_kernel(place, act, block0, block1, block2, block3, out):
    x_index = place[0]
    count = act.shape[0]
    dims = (((1,), (1,)), ((), ()))
    units = act.shape[2]
    joined = [jnp.concatenate([act[z], act[z + 1]], axis=1) for z in range(0, count, 2)]
    for step, block in enumerate((block0, block1, block2, block3)):
        total = 0.0
        for z in range(count // 2):
            weight = block[:, 2 * z * units : 2 * (z + 1) * units]
            total += lax.dot_general(weight, joined[z], dims, preferred_element_type=F32)
        out[lax.rem(x_index + NX - step, NX)] = total.astype(BF16)


def down_product(place, act, blocks):
    count, slots, units = act.shape
    columns = blocks[0].shape[0]
    vmem = pl.BlockSpec(memory_space=pltpu.VMEM)
    return pl.pallas_call(
        down_kernel,
        out_shape=jax.ShapeDtypeStruct((NX, columns, slots), BF16),
        in_specs=[pl.BlockSpec(memory_space=pltpu.SMEM)] + [vmem] * 5,
        out_specs=vmem,
        compiler_params=pltpu.CompilerParams(vmem_limit_bytes=40 * 2**20),
        cost_estimate=pl.CostEstimate(
            flops=2 * slots * columns * NX * count * units, bytes_accessed=5 * 2**20, transcendentals=0
        ),
    )(place, act, *blocks)


def attend(queries, keys, values, lengths):
    group_rows, ctx_len, head_size = keys.shape
    query_heads = queries.reshape(group_rows, -1, head_size)
    scores = jnp.einsum("rhd,rjd->rhj", query_heads, keys, preferred_element_type=F32)
    scores = scores * head_size ** (-0.5)
    valid = jnp.arange(ctx_len, dtype=jnp.int32)[None, None, :] < lengths[:, None, None]
    scores = jnp.where(valid, scores, -1e30)
    highest = jnp.max(scores, axis=-1, keepdims=True)
    weights = jnp.exp(scores - highest)
    probs = (weights / jnp.sum(weights, axis=-1, keepdims=True)).astype(BF16)
    attn = jnp.einsum("rhj,rjd->rhd", probs, values, preferred_element_type=F32)
    return attn.astype(BF16).reshape(queries.shape)


def shards(
    queries,
    keys,
    values,
    lengths,
    out_weight,
    residual,
    norm_gain,
    routes,
    route_weight,
    up_weight,
    down_weight,
):
    experts = lax.axis_size(("pool", "tp"))
    block_index = lax.axis_index(("pool", "tp"))
    group_index = lax.axis_index("grp")
    x_index, member = group_index // (NZ * PAIR), group_index % PAIR
    rows, columns = residual.shape
    top_count = routes.shape[1]
    slot_cap = min(rows, rows * top_count * 2 // experts)
    slots = experts * slot_cap
    width = norm_gain.shape[0]
    units = up_weight.shape[2]
    parts = NX * PAIR

    own_routes = lax.dynamic_slice_in_dim(routes, block_index * rows, rows, 0)
    own_weight = lax.dynamic_slice_in_dim(route_weight, block_index * rows, rows, 0)
    named = own_routes.T[:, None, :] == jnp.arange(experts, dtype=jnp.int32)[None, :, None]
    weight_of = jnp.sum(jnp.where(named, own_weight.T[:, None, :], 0.0), axis=0)
    named = jnp.any(named, axis=0)
    earlier = jnp.arange(rows)[:, None] < jnp.arange(rows)[None, :]
    place = jnp.dot(named.astype(BF16), earlier.astype(BF16), preferred_element_type=F32)
    here = place.astype(jnp.int32)[:, None, :] == jnp.arange(slot_cap, dtype=jnp.int32)[None, :, None]
    here = jnp.logical_and(here, named[:, None, :])
    select = here.astype(BF16).reshape(slots, rows)
    combine = jnp.where(here, weight_of[:, None, :], 0.0).reshape(slots, rows)

    attn = attend(queries, keys, values, lengths)
    attn = spread(attn, NZ, "grp", GATHER)
    attn = spread(attn.reshape(-1, attn.shape[2]), parts, "grp", REDUCE)
    attn = attn.reshape(NX, PAIR, NZ, -1, attn.shape[2]).transpose(0, 2, 1, 3, 4)
    attn = attn.reshape(experts * rows, attn.shape[4])

    up_blocks, down_blocks = [], []
    for step in range(NX):
        wanted = (x_index + step) % NX
        block = lax.dynamic_slice_in_dim(up_weight[0], wanted * (width // NX), width // NX, 0)
        block = lax.ppermute(block, "grp", moves(step, 0)) if step else block
        up_blocks.append(block.reshape(NZ, PAIR, columns, units))
    sent = jnp.stack([lax.dynamic_index_in_dim(w, 1 - member, 1, keepdims=False) for w in up_blocks])
    projected = jnp.dot(attn, out_weight, preferred_element_type=F32).astype(BF16)
    projected, sent = lax.optimization_barrier((projected, sent))
    got = lax.ppermute(sent, "grp", moves(0, 1))
    projected = exchange(projected.reshape(experts, rows, columns), ("pool", "tp"))
    hidden = jnp.sum(projected.astype(F32), axis=0) + residual.astype(F32)
    hidden = hidden.astype(BF16)
    hidden, down_weight = lax.optimization_barrier((hidden, down_weight))
    for step in range(NX):
        wanted = (x_index + step) % NX
        block = lax.dynamic_slice_in_dim(down_weight[0], wanted * (8 * units), 8 * units, 1)
        down_blocks.append(lax.ppermute(block, "grp", moves(step, 0)) if step else block)

    slot_rows = jnp.dot(select, hidden, preferred_element_type=F32).astype(BF16)
    slot_rows = exchange(slot_rows.reshape(experts, slot_cap, columns), ("pool", "tp"))
    slot_rows = spread(slot_rows.reshape(slots, columns), NZ, "grp", GATHER)
    gain = norm_gain.reshape(NX, NZ, PAIR, columns)
    gain = lax.dynamic_index_in_dim(gain, x_index, 0, keepdims=False)
    gain = lax.dynamic_index_in_dim(gain, member, 1, keepdims=False)
    place = jnp.stack([x_index, member]).astype(jnp.int32)
    partial_up = up_product(place, slot_rows, gain, up_blocks, got)
    total_up = jnp.sum(exchange(partial_up, "grp", REDUCE).astype(F32), axis=0)
    count = slots // units
    squares = (total_up[slots : slots + count] + total_up[slots + count : slots + 2 * count]).reshape(slots, 1)
    scale = lax.rsqrt(squares / width + 1e-06)
    act = jax.nn.silu(total_up[:slots] * scale).astype(BF16)

    act = spread(act, 8, "grp", LINE)
    partial_out = exchange(down_product(place, act, down_blocks), "grp", CROSS)
    expert_out = jnp.sum(partial_out.astype(F32), axis=0).astype(BF16).T
    returned = exchange(expert_out.reshape(experts, slot_cap, columns), ("pool", "tp"))
    returned = returned.reshape(slots, columns)
    high = lax.reduce_precision(combine, 8, 7)
    dims = (((0,), (0,)), ((), ()))
    result = lax.dot_general(high.astype(BF16), returned, dims, preferred_element_type=F32)
    result += lax.dot_general((combine - high).astype(BF16), returned, dims, preferred_element_type=F32)
    return result.astype(BF16)


def solution(mesh):
    placed = (
        P("grp", ("pool", "tp")),
        P("grp", None, None),
        P("grp", None, None),
        P("grp"),
        P(("pool", "tp"), "grp"),
        P(("pool", "tp"), "grp"),
        P(),
        P(),
        P(),
        P(("pool", "tp"), None, "grp"),
        P(("pool", "tp"), "grp", None),
    )
    return jax.shard_map(
        shards, mesh=mesh, in_specs=placed, out_specs=P(("pool", "tp"), "grp"), check_vma=False
    )
```

```python
import jax
import jax.numpy as jnp
from jax import lax
from jax.experimental import pallas as pl
from jax.experimental.pallas import tpu as pltpu
from jax.sharding import PartitionSpec as P

BF16 = jnp.bfloat16
F32 = jnp.float32
NX, NZ, PAIR = 4, 4, 2
GATHER = [[x * 8 + z * 2 + m for z in range(NZ)] for x in range(NX) for m in range(PAIR)]
LINE = [[x * 8 + z for z in range(8)] for x in range(NX)]
CROSS = [[x * 8 + z for x in range(NX)] for z in range(8)]
REDUCE = [[x * 8 + z * 2 + m for x in range(NX) for m in range(PAIR)] for z in range(NZ)]


def moves(by_x, by_member):
    return [
        (x * 8 + z * 2 + m, (x + by_x) % NX * 8 + z * 2 + (m + by_member) % PAIR)
        for x in range(NX)
        for z in range(NZ)
        for m in range(PAIR)
    ]


def spread(value, count, axis, groups=None):
    sent = jnp.broadcast_to(value[None], (count,) + value.shape)
    return lax.all_to_all(sent, axis, 0, 0, tiled=True, axis_index_groups=groups)


def exchange(value, axis, groups=None):
    return lax.all_to_all(value, axis, 0, 0, tiled=True, axis_index_groups=groups)


def up_kernel(place, rows, gain, block0, block1, block2, block3, got, got2, out):
    x_index, member = place[0], place[1]
    slots, units = rows.shape[1], out.shape[2]
    normed, squares = [], 0.0
    ones = jnp.ones((16, rows.shape[2]), BF16)
    dims = (((1,), (1,)), ((), ()))
    for z in range(NZ):
        value = rows[z].astype(F32)
        normed.append((value * gain[z][None, :]).astype(BF16))
        square = value * value
        high = square.astype(BF16)
        low = (square - high.astype(F32)).astype(BF16)
        squares += lax.dot_general(ones, high, dims, preferred_element_type=F32)
        squares += lax.dot_general(ones, low, dims, preferred_element_type=F32)
    row = lax.broadcasted_iota(jnp.int32, (16, units), 0)
    count = slots // units
    tail = jnp.zeros((16, units), F32)
    for i in range(count):
        part = squares[:, i * units : (i + 1) * units]
        high = part.astype(BF16).astype(F32)
        tail = jnp.where(row == i, high, tail)
        tail = jnp.where(row == count + i, part - high, tail)
    tail = tail.astype(BF16)
    for step, block in enumerate((block0, block1, block2, block3)):
        total = 0.0
        for z in range(NZ):
            other = got2[z] if step == 2 else got[min(step, 2), z]
            both = jnp.concatenate([block[z, member], other], axis=1)
            total += jnp.dot(normed[z], both, preferred_element_type=F32)
        total = total.astype(BF16)
        first = lax.rem(x_index + NX - step, NX) * PAIR
        for target, part in ((first + member, total[:, :units]), (first + 1 - member, total[:, units:])):
            out[target, :slots] = part
            out[target, slots:] = tail


def up_product(place, rows, gain, blocks, got, got2):
    slots, columns = rows.shape[1:]
    units = got.shape[3]
    vmem = pl.BlockSpec(memory_space=pltpu.VMEM)
    return pl.pallas_call(
        up_kernel,
        out_shape=jax.ShapeDtypeStruct((NX * PAIR, slots + 16, units), BF16),
        in_specs=[pl.BlockSpec(memory_space=pltpu.SMEM)] + [vmem] * 8,
        out_specs=vmem,
        compiler_params=pltpu.CompilerParams(vmem_limit_bytes=40 * 2**20),
        cost_estimate=pl.CostEstimate(
            flops=2 * slots * columns * NZ * NX * PAIR * units, bytes_accessed=6 * 2**20, transcendentals=0
        ),
    )(place, rows, gain, *blocks, got, got2)


def down_kernel(place, act, block0, block1, block2, block3, out):
    x_index = place[0]
    count = act.shape[0]
    dims = (((1,), (1,)), ((), ()))
    units = act.shape[2]
    joined = [jnp.concatenate([act[z], act[z + 1]], axis=1) for z in range(0, count, 2)]
    for step, block in enumerate((block0, block1, block2, block3)):
        total = 0.0
        for z in range(count // 2):
            weight = block[:, 2 * z * units : 2 * (z + 1) * units]
            total += lax.dot_general(weight, joined[z], dims, preferred_element_type=F32)
        out[lax.rem(x_index + NX - step, NX)] = total.astype(BF16)


def down_product(place, act, blocks):
    count, slots, units = act.shape
    columns = blocks[0].shape[0]
    vmem = pl.BlockSpec(memory_space=pltpu.VMEM)
    return pl.pallas_call(
        down_kernel,
        out_shape=jax.ShapeDtypeStruct((NX, columns, slots), BF16),
        in_specs=[pl.BlockSpec(memory_space=pltpu.SMEM)] + [vmem] * 5,
        out_specs=vmem,
        compiler_params=pltpu.CompilerParams(vmem_limit_bytes=40 * 2**20),
        cost_estimate=pl.CostEstimate(
            flops=2 * slots * columns * NX * count * units, bytes_accessed=5 * 2**20, transcendentals=0
        ),
    )(place, act, *blocks)


def attend(queries, keys, values, lengths):
    group_rows, ctx_len, head_size = keys.shape
    query_heads = queries.reshape(group_rows, -1, head_size)
    scores = jnp.einsum("rhd,rjd->rhj", query_heads, keys, preferred_element_type=F32)
    scores = scores * head_size ** (-0.5)
    valid = jnp.arange(ctx_len, dtype=jnp.int32)[None, None, :] < lengths[:, None, None]
    scores = jnp.where(valid, scores, -1e30)
    highest = jnp.max(scores, axis=-1, keepdims=True)
    weights = jnp.exp(scores - highest)
    probs = (weights / jnp.sum(weights, axis=-1, keepdims=True)).astype(BF16)
    attn = jnp.einsum("rhj,rjd->rhd", probs, values, preferred_element_type=F32)
    return attn.astype(BF16).reshape(queries.shape)


def shards(
    queries,
    keys,
    values,
    lengths,
    out_weight,
    residual,
    norm_gain,
    routes,
    route_weight,
    up_weight,
    down_weight,
):
    experts = lax.axis_size(("pool", "tp"))
    block_index = lax.axis_index(("pool", "tp"))
    group_index = lax.axis_index("grp")
    x_index, member = group_index // (NZ * PAIR), group_index % PAIR
    rows, columns = residual.shape
    top_count = routes.shape[1]
    slot_cap = min(rows, rows * top_count * 2 // experts)
    slots = experts * slot_cap
    width = norm_gain.shape[0]
    units = up_weight.shape[2]
    parts = NX * PAIR

    own_routes = lax.dynamic_slice_in_dim(routes, block_index * rows, rows, 0)
    own_weight = lax.dynamic_slice_in_dim(route_weight, block_index * rows, rows, 0)
    named = own_routes.T[:, None, :] == jnp.arange(experts, dtype=jnp.int32)[None, :, None]
    weight_of = jnp.sum(jnp.where(named, own_weight.T[:, None, :], 0.0), axis=0)
    named = jnp.any(named, axis=0)
    earlier = jnp.arange(rows)[:, None] < jnp.arange(rows)[None, :]
    place = jnp.dot(named.astype(BF16), earlier.astype(BF16), preferred_element_type=F32)
    here = place.astype(jnp.int32)[:, None, :] == jnp.arange(slot_cap, dtype=jnp.int32)[None, :, None]
    here = jnp.logical_and(here, named[:, None, :])
    select = here.astype(BF16).reshape(slots, rows)
    combine = jnp.where(here, weight_of[:, None, :], 0.0).reshape(slots, rows)

    attn = attend(queries, keys, values, lengths)
    def up_block(step):
        wanted = (x_index + step) % NX
        block = lax.dynamic_slice_in_dim(up_weight[0], wanted * (width // NX), width // NX, 0)
        block = lax.ppermute(block, "grp", moves(step, 0)) if step else block
        return block.reshape(NZ, PAIR, columns, units)

    def down_block(step):
        wanted = (x_index + step) % NX
        block = lax.dynamic_slice_in_dim(down_weight[0], wanted * (8 * units), 8 * units, 1)
        return lax.ppermute(block, "grp", moves(step, 0)) if step else block

    def other_half(block):
        return lax.dynamic_index_in_dim(block, 1 - member, 1, keepdims=False)

    attn = spread(attn, NZ, "grp", GATHER)
    attn, up1, up3 = lax.optimization_barrier((attn, up_block(1), up_block(3)))
    attn = spread(attn.reshape(-1, attn.shape[2]), parts, "grp", REDUCE)
    attn = attn.reshape(NX, PAIR, NZ, -1, attn.shape[2]).transpose(0, 2, 1, 3, 4)
    attn = attn.reshape(experts * rows, attn.shape[4])
    projected = jnp.dot(attn, out_weight, preferred_element_type=F32).astype(BF16)

    up0 = up_block(0)
    got = lax.ppermute(jnp.stack([other_half(w) for w in (up0, up1, up3)]), "grp", moves(0, 1))
    projected = exchange(projected.reshape(experts, rows, columns), ("pool", "tp"))
    projected, up2, got = lax.optimization_barrier((projected, up_block(2), got))
    hidden = jnp.sum(projected.astype(F32), axis=0) + residual.astype(F32)
    hidden = hidden.astype(BF16)

    slot_rows = jnp.dot(select, hidden, preferred_element_type=F32).astype(BF16)
    slot_rows = exchange(slot_rows.reshape(experts, slot_cap, columns), ("pool", "tp"))
    got2 = lax.ppermute(other_half(up2), "grp", moves(0, 1))
    slot_rows, got2 = lax.optimization_barrier((slot_rows, got2))
    slot_rows = spread(slot_rows.reshape(slots, columns), NZ, "grp", GATHER)
    slot_rows, down1, down3 = lax.optimization_barrier((slot_rows, down_block(1), down_block(3)))
    gain = norm_gain.reshape(NX, NZ, PAIR, columns)
    gain = lax.dynamic_index_in_dim(gain, x_index, 0, keepdims=False)
    gain = lax.dynamic_index_in_dim(gain, member, 1, keepdims=False)
    place = jnp.stack([x_index, member]).astype(jnp.int32)
    partial_up = up_product(place, slot_rows, gain, (up0, up1, up2, up3), got, got2)
    total_up = jnp.sum(exchange(partial_up, "grp", REDUCE).astype(F32), axis=0)
    count = slots // units
    squares = (total_up[slots : slots + count] + total_up[slots + count : slots + 2 * count]).reshape(slots, 1)
    scale = lax.rsqrt(squares / width + 1e-06)
    act = jax.nn.silu(total_up[:slots] * scale).astype(BF16)

    act = spread(act, 8, "grp", LINE)
    partial_out = exchange(down_product(place, act, (down_block(0), down1, down_block(2), down3)), "grp", CROSS)
    expert_out = jnp.sum(partial_out.astype(F32), axis=0).astype(BF16).T
    returned = exchange(expert_out.reshape(experts, slot_cap, columns), ("pool", "tp"))
    returned = returned.reshape(slots, columns)
    high = lax.reduce_precision(combine, 8, 7)
    dims = (((0,), (0,)), ((), ()))
    result = lax.dot_general(high.astype(BF16), returned, dims, preferred_element_type=F32)
    result += lax.dot_general((combine - high).astype(BF16), returned, dims, preferred_element_type=F32)
    return result.astype(BF16)


def solution(mesh):
    placed = (
        P("grp", ("pool", "tp")),
        P("grp", None, None),
        P("grp", None, None),
        P("grp"),
        P(("pool", "tp"), "grp"),
        P(("pool", "tp"), "grp"),
        P(),
        P(),
        P(),
        P(("pool", "tp"), None, "grp"),
        P(("pool", "tp"), "grp", None),
    )
    return jax.shard_map(
        shards, mesh=mesh, in_specs=placed, out_specs=P(("pool", "tp"), "grp"), check_vma=False
    )
```

```python
import jax
import jax.numpy as jnp
from jax import lax
from jax.experimental import pallas as pl
from jax.experimental.pallas import tpu as pltpu
from jax.sharding import PartitionSpec as P

BF16 = jnp.bfloat16
F32 = jnp.float32
NX, NZ, PAIR = 4, 4, 2
GATHER = [[x * 8 + z * 2 + m for z in range(NZ)] for x in range(NX) for m in range(PAIR)]
LINE = [[x * 8 + z for z in range(8)] for x in range(NX)]
CROSS = [[x * 8 + z for x in range(NX)] for z in range(8)]
REDUCE = [[x * 8 + z * 2 + m for x in range(NX) for m in range(PAIR)] for z in range(NZ)]


def moves(by_x, by_member):
    return [
        (x * 8 + z * 2 + m, (x + by_x) % NX * 8 + z * 2 + (m + by_member) % PAIR)
        for x in range(NX)
        for z in range(NZ)
        for m in range(PAIR)
    ]


def spread(value, count, axis, groups=None):
    sent = jnp.broadcast_to(value[None], (count,) + value.shape)
    return lax.all_to_all(sent, axis, 0, 0, tiled=True, axis_index_groups=groups)


def exchange(value, axis, groups=None):
    return lax.all_to_all(value, axis, 0, 0, tiled=True, axis_index_groups=groups)


def whole(count):
    return [pl.BlockSpec(memory_space=pltpu.VMEM)] * count


PARAMS = pltpu.CompilerParams(vmem_limit_bytes=40 * 2**20)


def project_kernel(attn, weight, out):
    run = attn.shape[2]
    for x in range(NX):
        value = jnp.concatenate(
            [attn[x * PAIR + m].reshape(NZ * run, attn.shape[3]) for m in range(PAIR)], axis=0
        )
        value = jnp.dot(value, weight[...], preferred_element_type=F32).astype(BF16)
        for m in range(PAIR):
            for z in range(NZ):
                first = (m * NZ + z) * run
                out[x * NZ + z, m * run : (m + 1) * run] = value[first : first + run]


def project(attn, weight):
    rows, columns = PAIR * attn.shape[2], weight.shape[1]
    return pl.pallas_call(
        project_kernel,
        out_shape=jax.ShapeDtypeStruct((NX * NZ, rows, columns), BF16),
        in_specs=whole(2),
        out_specs=whole(1)[0],
        compiler_params=PARAMS,
        cost_estimate=pl.CostEstimate(
            flops=2 * NX * NZ * rows * columns * weight.shape[0], bytes_accessed=2 * 2**20, transcendentals=0
        ),
    )(attn, weight)


def head_sum_kernel(parts, residual, select, out):
    total = residual[...].astype(F32)
    for i in range(parts.shape[0]):
        total += parts[i].astype(F32)
    out[...] = jnp.dot(select[...], total.astype(BF16), preferred_element_type=F32).astype(BF16)


def head_sum(parts, residual, select):
    slots, columns = select.shape[0], residual.shape[1]
    return pl.pallas_call(
        head_sum_kernel,
        out_shape=jax.ShapeDtypeStruct((slots, columns), BF16),
        in_specs=whole(3),
        out_specs=whole(1)[0],
        compiler_params=PARAMS,
        cost_estimate=pl.CostEstimate(
            flops=2 * slots * columns * residual.shape[0], bytes_accessed=2**20, transcendentals=0
        ),
    )(parts, residual, select)


def up_kernel(place, rows, gain, own, got, left, far, right, out):
    x_index, member = place[0], place[1]
    slots, units = rows.shape[2], out.shape[2]
    depth = NZ * rows.shape[1]
    value = rows[...].astype(F32).reshape(depth, slots)
    squares = jnp.sum(value * value, axis=0, keepdims=True)
    normed = (value * gain[...]).astype(BF16).T
    row = lax.broadcasted_iota(jnp.int32, (16, units), 0)
    count = slots // units
    tail = jnp.zeros((16, units), F32)
    for i in range(count):
        part = jnp.broadcast_to(squares[:, i * units : (i + 1) * units], (16, units))
        high = part.astype(BF16).astype(F32)
        tail = jnp.where(row == i, high, tail)
        tail = jnp.where(row == count + i, part - high, tail)
    tail = tail.astype(BF16)
    blocks = [(own[x_index], got[x_index])] + [(b[0], b[1]) for b in (left, far, right)]
    for step, block in enumerate(blocks):
        total = jnp.dot(normed, jnp.concatenate(block, axis=1), preferred_element_type=F32).astype(BF16)
        first = lax.rem(x_index + NX - step, NX) * PAIR
        for target, part in ((first + member, total[:, :units]), (first + 1 - member, total[:, units:])):
            out[target, :slots] = part
            out[target, slots:] = tail


def up_product(place, rows, gain, blocks):
    columns, slots = rows.shape[1:]
    units = blocks[0].shape[2]
    return pl.pallas_call(
        up_kernel,
        out_shape=jax.ShapeDtypeStruct((NX * PAIR, slots + 16, units), BF16),
        in_specs=[pl.BlockSpec(memory_space=pltpu.SMEM)] + whole(7),
        out_specs=whole(1)[0],
        compiler_params=PARAMS,
        cost_estimate=pl.CostEstimate(
            flops=2 * slots * columns * NZ * NX * PAIR * units, bytes_accessed=6 * 2**20, transcendentals=0
        ),
    )(place, rows, gain, *blocks)


def down_kernel(place, act, block0, block1, block2, block3, out):
    x_index = place[0]
    count, units = act.shape[0], act.shape[2]
    dims = (((1,), (1,)), ((), ()))
    joined = [jnp.concatenate([act[z], act[z + 1]], axis=1) for z in range(0, count, 2)]
    for step, block in enumerate((block0, block1, block2, block3)):
        total = 0.0
        for z in range(count // 2):
            weight = block[:, 2 * z * units : 2 * (z + 1) * units]
            total += lax.dot_general(weight, joined[z], dims, preferred_element_type=F32)
        out[lax.rem(x_index + NX - step, NX)] = total.astype(BF16)


def down_product(place, act, blocks):
    count, slots, units = act.shape
    columns = blocks[0].shape[0]
    return pl.pallas_call(
        down_kernel,
        out_shape=jax.ShapeDtypeStruct((NX, columns, slots), BF16),
        in_specs=[pl.BlockSpec(memory_space=pltpu.SMEM)] + whole(5),
        out_specs=whole(1)[0],
        compiler_params=PARAMS,
        cost_estimate=pl.CostEstimate(
            flops=2 * slots * columns * NX * count * units, bytes_accessed=5 * 2**20, transcendentals=0
        ),
    )(place, act, *blocks)


def attend(queries, keys, values, lengths):
    group_rows, ctx_len, head_size = keys.shape
    query_heads = queries.reshape(group_rows, -1, head_size)
    scores = jnp.einsum("rhd,rjd->rhj", query_heads, keys, preferred_element_type=F32)
    scores = scores * head_size ** (-0.5)
    valid = jnp.arange(ctx_len, dtype=jnp.int32)[None, None, :] < lengths[:, None, None]
    scores = jnp.where(valid, scores, -1e30)
    highest = jnp.max(scores, axis=-1, keepdims=True)
    weights = jnp.exp(scores - highest)
    probs = (weights / jnp.sum(weights, axis=-1, keepdims=True)).astype(BF16)
    attn = jnp.einsum("rhj,rjd->rhd", probs, values, preferred_element_type=F32)
    return attn.astype(BF16).reshape(queries.shape)


def shards(
    queries,
    keys,
    values,
    lengths,
    out_weight,
    residual,
    norm_gain,
    routes,
    route_weight,
    up_weight,
    down_weight,
):
    experts = lax.axis_size(("pool", "tp"))
    block_index = lax.axis_index(("pool", "tp"))
    group_index = lax.axis_index("grp")
    x_index, member = group_index // (NZ * PAIR), group_index % PAIR
    rows, columns = residual.shape
    top_count = routes.shape[1]
    slot_cap = min(rows, rows * top_count * 2 // experts)
    slots = experts * slot_cap
    width = norm_gain.shape[0]
    units = up_weight.shape[2]
    parts = NX * PAIR

    own_routes = lax.dynamic_slice_in_dim(routes, block_index * rows, rows, 0)
    own_weight = lax.dynamic_slice_in_dim(route_weight, block_index * rows, rows, 0)
    named = own_routes.T[:, None, :] == jnp.arange(experts, dtype=jnp.int32)[None, :, None]
    weight_of = jnp.sum(jnp.where(named, own_weight.T[:, None, :], 0.0), axis=0)
    named = jnp.any(named, axis=0)
    earlier = jnp.arange(rows)[:, None] < jnp.arange(rows)[None, :]
    place = jnp.dot(named.astype(BF16), earlier.astype(BF16), preferred_element_type=F32)
    here = place.astype(jnp.int32)[:, None, :] == jnp.arange(slot_cap, dtype=jnp.int32)[None, :, None]
    here = jnp.logical_and(here, named[:, None, :])
    select = here.astype(BF16).reshape(slots, rows)
    combine = jnp.where(here, weight_of[:, None, :], 0.0).reshape(slots, rows)

    attn = attend(queries, keys, values, lengths)

    def up_half(which):
        up_parts = up_weight[0].reshape(NX, NZ, PAIR, columns, units)
        half = lax.dynamic_index_in_dim(up_parts, which, 2, keepdims=False)
        return half.reshape(NX, NZ * columns, units)

    def up_block(step):
        wanted = (x_index + step) % NX
        block = [lax.dynamic_index_in_dim(w, wanted, 0, keepdims=False) for w in (own, got)]
        return lax.ppermute(jnp.stack(block), "grp", moves(step, 0))

    def down_block(step):
        wanted = (x_index + step) % NX
        block = lax.dynamic_slice_in_dim(down_weight[0], wanted * (8 * units), 8 * units, 1)
        return lax.ppermute(block, "grp", moves(step, 0)) if step else block

    attn = spread(attn, NZ, "grp", GATHER)
    attn = spread(attn.reshape(-1, attn.shape[2]), parts, "grp", REDUCE)
    attn, up_weight = lax.optimization_barrier((attn, up_weight))
    projected = project(attn.reshape(parts, NZ, -1, attn.shape[2]), out_weight)
    projected = exchange(projected, ("pool", "tp"))
    own, got = up_half(member), lax.ppermute(up_half(1 - member), "grp", moves(0, 1))
    projected, got = lax.optimization_barrier((projected, got))
    slot_rows = head_sum(projected, residual, select)
    slot_rows = exchange(slot_rows.reshape(experts, slot_cap, columns), ("pool", "tp"))
    slot_rows, own, got = lax.optimization_barrier((slot_rows, own, got))
    slot_rows = spread(slot_rows.reshape(slots, columns).T, NZ, "grp", GATHER)
    gain = norm_gain.reshape(NX, NZ, PAIR, columns)
    gain = lax.dynamic_index_in_dim(gain, x_index, 0, keepdims=False)
    gain = lax.dynamic_index_in_dim(gain, member, 1, keepdims=False).reshape(NZ * columns, 1)
    place = jnp.stack([x_index, member]).astype(jnp.int32)
    partial_up = up_product(place, slot_rows, gain, (own, got, up_block(1), up_block(2), up_block(3)))
    total_up = jnp.sum(exchange(partial_up, "grp", REDUCE).astype(F32), axis=0)
    count = slots // units
    squares = (total_up[slots : slots + count] + total_up[slots + count : slots + 2 * count]).reshape(slots, 1)
    scale = lax.rsqrt(squares / width + 1e-06)
    act = jax.nn.silu(total_up[:slots] * scale).astype(BF16)

    act, down_weight = lax.optimization_barrier((act, down_weight))
    act = spread(act, 8, "grp", LINE)
    partial_out = exchange(down_product(place, act, [down_block(step) for step in range(NX)]), "grp", CROSS)
    expert_out = jnp.sum(partial_out.astype(F32), axis=0).astype(BF16).T
    returned = exchange(expert_out.reshape(experts, slot_cap, columns), ("pool", "tp"))
    returned = returned.reshape(slots, columns)
    high = lax.reduce_precision(combine, 8, 7)
    dims = (((0,), (0,)), ((), ()))
    result = lax.dot_general(high.astype(BF16), returned, dims, preferred_element_type=F32)
    result += lax.dot_general((combine - high).astype(BF16), returned, dims, preferred_element_type=F32)
    return result.astype(BF16)


def solution(mesh):
    placed = (
        P("grp", ("pool", "tp")),
        P("grp", None, None),
        P("grp", None, None),
        P("grp"),
        P(("pool", "tp"), "grp"),
        P(("pool", "tp"), "grp"),
        P(),
        P(),
        P(),
        P(("pool", "tp"), None, "grp"),
        P(("pool", "tp"), "grp", None),
    )
    return jax.shard_map(
        shards, mesh=mesh, in_specs=placed, out_specs=P(("pool", "tp"), "grp"), check_vma=False
    )
```

```python
import jax
import jax.numpy as jnp
from jax import lax
from jax.experimental import pallas as pl
from jax.experimental.pallas import tpu as pltpu
from jax.sharding import PartitionSpec as P

BF16 = jnp.bfloat16
F32 = jnp.float32
NX, NZ, PAIR = 4, 4, 2
GATHER = [[x * 8 + z * 2 + m for z in range(NZ)] for x in range(NX) for m in range(PAIR)]
LINE = [[x * 8 + z for z in range(8)] for x in range(NX)]
CROSS = [[x * 8 + z for x in range(NX)] for z in range(8)]
REDUCE = [[x * 8 + z * 2 + m for x in range(NX) for m in range(PAIR)] for z in range(NZ)]


def moves(by_x, by_member):
    return [
        (x * 8 + z * 2 + m, (x + by_x) % NX * 8 + z * 2 + (m + by_member) % PAIR)
        for x in range(NX)
        for z in range(NZ)
        for m in range(PAIR)
    ]


def spread(value, count, axis, groups=None):
    sent = jnp.broadcast_to(value[None], (count,) + value.shape)
    return lax.all_to_all(sent, axis, 0, 0, tiled=True, axis_index_groups=groups)


def exchange(value, axis, groups=None):
    return lax.all_to_all(value, axis, 0, 0, tiled=True, axis_index_groups=groups)


def whole(count):
    return [pl.BlockSpec(memory_space=pltpu.VMEM)] * count


PARAMS = pltpu.CompilerParams(vmem_limit_bytes=40 * 2**20)


def project_kernel(attn, weight, out):
    run = attn.shape[2]
    dims = (((1,), (1,)), ((), ()))
    for x in range(NX):
        value = jnp.concatenate(
            [attn[x * PAIR + m].reshape(NZ * run, attn.shape[3]) for m in range(PAIR)], axis=0
        )
        value = lax.dot_general(value, weight[...], dims, preferred_element_type=F32).astype(BF16)
        for m in range(PAIR):
            for z in range(NZ):
                first = (m * NZ + z) * run
                out[x * NZ + z, m * run : (m + 1) * run] = value[first : first + run]


def project(attn, weight):
    rows, columns = PAIR * attn.shape[2], weight.shape[0]
    return pl.pallas_call(
        project_kernel,
        out_shape=jax.ShapeDtypeStruct((NX * NZ, rows, columns), BF16),
        in_specs=whole(2),
        out_specs=whole(1)[0],
        compiler_params=PARAMS,
        cost_estimate=pl.CostEstimate(
            flops=2 * NX * NZ * rows * columns * weight.shape[1], bytes_accessed=2 * 2**20, transcendentals=0
        ),
    )(attn, weight)


def head_sum_kernel(parts, residual, select, out):
    total = residual[...].astype(F32)
    for i in range(parts.shape[0]):
        total += parts[i].astype(F32)
    out[...] = jnp.dot(select[...], total.astype(BF16), preferred_element_type=F32).astype(BF16)


def head_sum(parts, residual, select):
    slots, columns = select.shape[0], residual.shape[1]
    return pl.pallas_call(
        head_sum_kernel,
        out_shape=jax.ShapeDtypeStruct((slots, columns), BF16),
        in_specs=whole(3),
        out_specs=whole(1)[0],
        compiler_params=PARAMS,
        cost_estimate=pl.CostEstimate(
            flops=2 * slots * columns * residual.shape[0], bytes_accessed=2**20, transcendentals=0
        ),
    )(parts, residual, select)


def up_kernel(place, rows, gain, block0, block1, block2, block3, out):
    x_index = place[0]
    slots, units = rows.shape[2], out.shape[2]
    value = rows[...].reshape(rows.shape[0] * rows.shape[1], slots)
    squares = jnp.sum(jnp.square(value.astype(F32)), axis=0, keepdims=True)
    normed = (value.T.astype(F32) * gain[...]).astype(BF16)
    row = lax.broadcasted_iota(jnp.int32, (16, units), 0)
    count = slots // units
    tail = jnp.zeros((16, units), F32)
    for i in range(count):
        part = jnp.broadcast_to(squares[:, i * units : (i + 1) * units], (16, units))
        high = part.astype(BF16).astype(F32)
        tail = jnp.where(row == i, high, tail)
        tail = jnp.where(row == count + i, part - high, tail)
    tail = tail.astype(BF16)
    for step, block in ((0, (block0, block1)), (2, (block2, block3))):
        weight = jnp.concatenate([b[...] for b in block], axis=1)
        total = jnp.dot(normed, weight, preferred_element_type=F32).astype(BF16)
        for i in range(2):
            target = lax.rem(x_index + NX - step - i, NX)
            out[target, :slots] = total[:, i * units : (i + 1) * units]
            out[target, slots:] = tail


def up_product(place, rows, gain, blocks):
    count, columns, slots = rows.shape
    units = blocks[0].shape[1]
    return pl.pallas_call(
        up_kernel,
        out_shape=jax.ShapeDtypeStruct((NX, slots + 16, units), BF16),
        in_specs=[pl.BlockSpec(memory_space=pltpu.SMEM)] + whole(6),
        out_specs=whole(1)[0],
        compiler_params=PARAMS,
        cost_estimate=pl.CostEstimate(
            flops=2 * slots * columns * count * NX * units, bytes_accessed=6 * 2**20, transcendentals=0
        ),
    )(place, rows, gain, *blocks)


def down_kernel(place, act, block0, block1, block2, block3, out):
    x_index = place[0]
    count, units = act.shape[0], act.shape[2]
    dims = (((1,), (1,)), ((), ()))
    joined = [jnp.concatenate([act[z], act[z + 1]], axis=1) for z in range(0, count, 2)]
    for step, block in enumerate((block0, block1, block2, block3)):
        total = 0.0
        for z in range(count // 2):
            weight = block[:, 2 * z * units : 2 * (z + 1) * units]
            total += lax.dot_general(weight, joined[z], dims, preferred_element_type=F32)
        out[lax.rem(x_index + NX - step, NX)] = total.astype(BF16)


def down_product(place, act, blocks):
    count, slots, units = act.shape
    columns = blocks[0].shape[0]
    return pl.pallas_call(
        down_kernel,
        out_shape=jax.ShapeDtypeStruct((NX, columns, slots), BF16),
        in_specs=[pl.BlockSpec(memory_space=pltpu.SMEM)] + whole(5),
        out_specs=whole(1)[0],
        compiler_params=PARAMS,
        cost_estimate=pl.CostEstimate(
            flops=2 * slots * columns * NX * count * units, bytes_accessed=5 * 2**20, transcendentals=0
        ),
    )(place, act, *blocks)


def attend(queries, keys, values, lengths):
    group_rows, ctx_len, head_size = keys.shape
    query_heads = queries.reshape(group_rows, -1, head_size)
    scores = jnp.einsum("rhd,rjd->rhj", query_heads, keys, preferred_element_type=F32)
    scores = scores * head_size ** (-0.5)
    valid = jnp.arange(ctx_len, dtype=jnp.int32)[None, None, :] < lengths[:, None, None]
    scores = jnp.where(valid, scores, -1e30)
    highest = jnp.max(scores, axis=-1, keepdims=True)
    weights = jnp.exp(scores - highest)
    probs = (weights / jnp.sum(weights, axis=-1, keepdims=True)).astype(BF16)
    attn = jnp.einsum("rhj,rjd->rhd", probs, values, preferred_element_type=F32)
    return attn.astype(BF16).reshape(queries.shape)


def shards(
    queries,
    keys,
    values,
    lengths,
    out_weight,
    residual,
    norm_gain,
    routes,
    route_weight,
    up_weight,
    down_weight,
):
    experts = lax.axis_size(("pool", "tp"))
    block_index = lax.axis_index(("pool", "tp"))
    group_index = lax.axis_index("grp")
    x_index = group_index // (NZ * PAIR)
    rows, columns = residual.shape
    top_count = routes.shape[1]
    slot_cap = min(rows, rows * top_count * 2 // experts)
    slots = experts * slot_cap
    width = norm_gain.shape[0]
    units = up_weight.shape[2]
    parts = NX * PAIR

    own_routes = lax.dynamic_slice_in_dim(routes, block_index * rows, rows, 0)
    own_weight = lax.dynamic_slice_in_dim(route_weight, block_index * rows, rows, 0)
    named = own_routes.T[:, None, :] == jnp.arange(experts, dtype=jnp.int32)[None, :, None]
    weight_of = jnp.sum(jnp.where(named, own_weight.T[:, None, :], 0.0), axis=0)
    named = jnp.any(named, axis=0)
    earlier = jnp.arange(rows)[:, None] < jnp.arange(rows)[None, :]
    place = jnp.dot(named.astype(BF16), earlier.astype(BF16), preferred_element_type=F32)
    here = place.astype(jnp.int32)[:, None, :] == jnp.arange(slot_cap, dtype=jnp.int32)[None, :, None]
    here = jnp.logical_and(here, named[:, None, :])
    select = here.astype(BF16).reshape(slots, rows)
    combine = jnp.where(here, weight_of[:, None, :], 0.0).reshape(slots, rows)

    attn = attend(queries, keys, values, lengths)
    def up_block(step):
        wanted = (x_index + step) % NX
        block = lax.dynamic_slice_in_dim(up_weight[0], wanted * (width // NX), width // NX, 0)
        return lax.ppermute(block, "grp", moves(step, 0)) if step else block

    def down_block(step):
        wanted = (x_index + step) % NX
        block = lax.dynamic_slice_in_dim(down_weight[0], wanted * (8 * units), 8 * units, 1)
        return lax.ppermute(block, "grp", moves(step, 0)) if step else block

    attn = spread(attn, NZ, "grp", GATHER)
    attn = spread(attn.reshape(-1, attn.shape[2]), parts, "grp", REDUCE)
    projected = project(attn.reshape(parts, NZ, -1, attn.shape[2]), out_weight.T)
    projected, down_weight = lax.optimization_barrier((projected, down_weight))
    projected = exchange(projected, ("pool", "tp"))
    projected, down1, down3 = lax.optimization_barrier((projected, down_block(1), down_block(3)))
    slot_rows = head_sum(projected, residual, select)
    slot_rows = exchange(slot_rows.reshape(experts, slot_cap, columns), ("pool", "tp"))
    slot_rows, up_weight = lax.optimization_barrier((slot_rows, up_weight))
    slot_rows = spread(slot_rows.reshape(slots, columns).T, 8, "grp", LINE)
    gain = lax.dynamic_slice_in_dim(norm_gain, x_index * (width // NX), width // NX, 0)[None, :]
    place = x_index.astype(jnp.int32)[None]
    partial_up = up_product(place, slot_rows, gain, [up_block(step) for step in range(NX)])
    total_up = jnp.sum(exchange(partial_up, "grp", CROSS).astype(F32), axis=0)
    count = slots // units
    squares = (total_up[slots : slots + count] + total_up[slots + count : slots + 2 * count]).reshape(slots, 1)
    scale = lax.rsqrt(squares / width + 1e-06)
    act = jax.nn.silu(total_up[:slots] * scale).astype(BF16)

    act, down_weight = lax.optimization_barrier((act, down_weight))
    act = spread(act, 8, "grp", LINE)
    partial_out = exchange(down_product(place, act, (down_block(0), down1, down_block(2), down3)), "grp", CROSS)
    expert_out = jnp.sum(partial_out.astype(F32), axis=0).astype(BF16).T
    returned = exchange(expert_out.reshape(experts, slot_cap, columns), ("pool", "tp"))
    returned = returned.reshape(slots, columns)
    high = lax.reduce_precision(combine, 8, 7)
    dims = (((0,), (0,)), ((), ()))
    result = lax.dot_general(high.astype(BF16), returned, dims, preferred_element_type=F32)
    result += lax.dot_general((combine - high).astype(BF16), returned, dims, preferred_element_type=F32)
    return result.astype(BF16)


def solution(mesh):
    placed = (
        P("grp", ("pool", "tp")),
        P("grp", None, None),
        P("grp", None, None),
        P("grp"),
        P(("pool", "tp"), "grp"),
        P(("pool", "tp"), "grp"),
        P(),
        P(),
        P(),
        P(("pool", "tp"), None, "grp"),
        P(("pool", "tp"), "grp", None),
    )
    return jax.shard_map(
        shards, mesh=mesh, in_specs=placed, out_specs=P(("pool", "tp"), "grp"), check_vma=False
    )
```

```python
import jax
import jax.numpy as jnp
from jax import lax
from jax.experimental import pallas as pl
from jax.experimental.pallas import tpu as pltpu
from jax.sharding import PartitionSpec as P

BF16 = jnp.bfloat16
F32 = jnp.float32
NX, NZ, PAIR = 4, 4, 2
GATHER = [[x * 8 + z * 2 + m for z in range(NZ)] for x in range(NX) for m in range(PAIR)]
LINE = [[x * 8 + z for z in range(8)] for x in range(NX)]
CROSS = [[x * 8 + z for x in range(NX)] for z in range(8)]
REDUCE = [[x * 8 + z * 2 + m for x in range(NX) for m in range(PAIR)] for z in range(NZ)]


def moves(by_x, by_member):
    return [
        (x * 8 + z * 2 + m, (x + by_x) % NX * 8 + z * 2 + (m + by_member) % PAIR)
        for x in range(NX)
        for z in range(NZ)
        for m in range(PAIR)
    ]


def turns(by):
    return [(x * 8 + z, x * 8 + (z + by) % 8) for x in range(NX) for z in range(8)]


def spread(value, count, axis, groups=None):
    sent = jnp.broadcast_to(value[None], (count,) + value.shape)
    return lax.all_to_all(sent, axis, 0, 0, tiled=True, axis_index_groups=groups)


def exchange(value, axis, groups=None):
    return lax.all_to_all(value, axis, 0, 0, tiled=True, axis_index_groups=groups)


def whole(count):
    return [pl.BlockSpec(memory_space=pltpu.VMEM)] * count


PARAMS = pltpu.CompilerParams(vmem_limit_bytes=40 * 2**20)


def project_kernel(attn, weight, out):
    run = attn.shape[2]
    dims = (((1,), (1,)), ((), ()))
    for x in range(NX):
        value = jnp.concatenate(
            [attn[x * PAIR + m].reshape(NZ * run, attn.shape[3]) for m in range(PAIR)], axis=0
        )
        value = lax.dot_general(value, weight[...], dims, preferred_element_type=F32).astype(BF16)
        for m in range(PAIR):
            for z in range(NZ):
                first = (m * NZ + z) * run
                out[x * NZ + z, m * run : (m + 1) * run] = value[first : first + run]


def project(attn, weight):
    rows, columns = PAIR * attn.shape[2], weight.shape[0]
    return pl.pallas_call(
        project_kernel,
        out_shape=jax.ShapeDtypeStruct((NX * NZ, rows, columns), BF16),
        in_specs=whole(2),
        out_specs=whole(1)[0],
        compiler_params=PARAMS,
        cost_estimate=pl.CostEstimate(
            flops=2 * NX * NZ * rows * columns * weight.shape[1], bytes_accessed=2 * 2**20, transcendentals=0
        ),
    )(attn, weight)


def head_sum_kernel(parts, residual, select, out):
    total = residual[...].astype(F32)
    for i in range(parts.shape[0]):
        total += parts[i].astype(F32)
    out[...] = jnp.dot(select[...], total.astype(BF16), preferred_element_type=F32).astype(BF16)


def head_sum(parts, residual, select):
    slots, columns = select.shape[0], residual.shape[1]
    return pl.pallas_call(
        head_sum_kernel,
        out_shape=jax.ShapeDtypeStruct((slots, columns), BF16),
        in_specs=whole(3),
        out_specs=whole(1)[0],
        compiler_params=PARAMS,
        cost_estimate=pl.CostEstimate(
            flops=2 * slots * columns * residual.shape[0], bytes_accessed=2**20, transcendentals=0
        ),
    )(parts, residual, select)


def up_kernel(place, same, before, after, gain, block0, block1, block2, block3, out):
    x_index, member = place[0], place[1]
    slots, units = same.shape[2], out.shape[2]
    depth = NZ * same.shape[1]
    other = jnp.concatenate([r[...].reshape(depth // 2, slots) for r in (before, after)], axis=0)
    normed, squares = [], 0.0
    for i, value in enumerate((same[...].reshape(depth, slots), other)):
        squares += jnp.sum(jnp.square(value.astype(F32)), axis=0, keepdims=True)
        normed.append((value.T.astype(F32) * gain[i : i + 1, :]).astype(BF16))
    row = lax.broadcasted_iota(jnp.int32, (16, units), 0)
    count = slots // units
    tail = jnp.zeros((16, units), F32)
    for i in range(count):
        part = jnp.broadcast_to(squares[:, i * units : (i + 1) * units], (16, units))
        high = part.astype(BF16).astype(F32)
        tail = jnp.where(row == i, high, tail)
        tail = jnp.where(row == count + i, part - high, tail)
    tail = tail.astype(BF16)
    for step, block in ((0, (block0, block1)), (2, (block2, block3))):
        total = 0.0
        for value, which in zip(normed, (member, 1 - member)):
            weight = jnp.concatenate([b[:, which].reshape(depth, units) for b in block], axis=1)
            total += jnp.dot(value, weight, preferred_element_type=F32)
        total = total.astype(BF16)
        for i in range(2):
            target = lax.rem(x_index + NX - step - i, NX)
            out[target, :slots] = total[:, i * units : (i + 1) * units]
            out[target, slots:] = tail


def up_product(place, rows, gain, blocks):
    count, columns, slots = rows[0].shape
    units = blocks[0].shape[3]
    return pl.pallas_call(
        up_kernel,
        out_shape=jax.ShapeDtypeStruct((NX, slots + 16, units), BF16),
        in_specs=[pl.BlockSpec(memory_space=pltpu.SMEM)] + whole(8),
        out_specs=whole(1)[0],
        compiler_params=PARAMS,
        cost_estimate=pl.CostEstimate(
            flops=4 * slots * columns * count * NX * units, bytes_accessed=6 * 2**20, transcendentals=0
        ),
    )(place, *rows, gain, *blocks)


def down_kernel(place, act, block0, block1, block2, block3, out):
    x_index = place[0]
    count, units = act.shape[0], act.shape[2]
    dims = (((1,), (1,)), ((), ()))
    joined = [jnp.concatenate([act[z], act[z + 1]], axis=1) for z in range(0, count, 2)]
    for step, block in enumerate((block0, block1, block2, block3)):
        total = 0.0
        for z in range(count // 2):
            weight = block[:, 2 * z * units : 2 * (z + 1) * units]
            total += lax.dot_general(weight, joined[z], dims, preferred_element_type=F32)
        out[lax.rem(x_index + NX - step, NX)] = total.astype(BF16)


def down_product(place, act, blocks):
    count, slots, units = act.shape
    columns = blocks[0].shape[0]
    return pl.pallas_call(
        down_kernel,
        out_shape=jax.ShapeDtypeStruct((NX, columns, slots), BF16),
        in_specs=[pl.BlockSpec(memory_space=pltpu.SMEM)] + whole(5),
        out_specs=whole(1)[0],
        compiler_params=PARAMS,
        cost_estimate=pl.CostEstimate(
            flops=2 * slots * columns * NX * count * units, bytes_accessed=5 * 2**20, transcendentals=0
        ),
    )(place, act, *blocks)


def attend(queries, keys, values, lengths):
    group_rows, ctx_len, head_size = keys.shape
    query_heads = queries.reshape(group_rows, -1, head_size)
    scores = jnp.einsum("rhd,rjd->rhj", query_heads, keys, preferred_element_type=F32)
    scores = scores * head_size ** (-0.5)
    valid = jnp.arange(ctx_len, dtype=jnp.int32)[None, None, :] < lengths[:, None, None]
    scores = jnp.where(valid, scores, -1e30)
    highest = jnp.max(scores, axis=-1, keepdims=True)
    weights = jnp.exp(scores - highest)
    probs = (weights / jnp.sum(weights, axis=-1, keepdims=True)).astype(BF16)
    attn = jnp.einsum("rhj,rjd->rhd", probs, values, preferred_element_type=F32)
    return attn.astype(BF16).reshape(queries.shape)


def shards(
    queries,
    keys,
    values,
    lengths,
    out_weight,
    residual,
    norm_gain,
    routes,
    route_weight,
    up_weight,
    down_weight,
):
    experts = lax.axis_size(("pool", "tp"))
    block_index = lax.axis_index(("pool", "tp"))
    group_index = lax.axis_index("grp")
    x_index, member = group_index // (NZ * PAIR), group_index % PAIR
    rows, columns = residual.shape
    top_count = routes.shape[1]
    slot_cap = min(rows, rows * top_count * 2 // experts)
    slots = experts * slot_cap
    width = norm_gain.shape[0]
    units = up_weight.shape[2]
    parts = NX * PAIR

    own_routes = lax.dynamic_slice_in_dim(routes, block_index * rows, rows, 0)
    own_weight = lax.dynamic_slice_in_dim(route_weight, block_index * rows, rows, 0)
    named = own_routes.T[:, None, :] == jnp.arange(experts, dtype=jnp.int32)[None, :, None]
    weight_of = jnp.sum(jnp.where(named, own_weight.T[:, None, :], 0.0), axis=0)
    named = jnp.any(named, axis=0)
    earlier = jnp.arange(rows)[:, None] < jnp.arange(rows)[None, :]
    place = jnp.dot(named.astype(BF16), earlier.astype(BF16), preferred_element_type=F32)
    here = place.astype(jnp.int32)[:, None, :] == jnp.arange(slot_cap, dtype=jnp.int32)[None, :, None]
    here = jnp.logical_and(here, named[:, None, :])
    select = here.astype(BF16).reshape(slots, rows)
    combine = jnp.where(here, weight_of[:, None, :], 0.0).reshape(slots, rows)

    attn = attend(queries, keys, values, lengths)
    def up_block(step):
        wanted = (x_index + step) % NX
        block = lax.dynamic_slice_in_dim(up_weight[0], wanted * (width // NX), width // NX, 0)
        block = lax.ppermute(block, "grp", moves(step, 0)) if step else block
        return block.reshape(NZ, PAIR, columns, units)

    def down_block(step):
        wanted = (x_index + step) % NX
        block = lax.dynamic_slice_in_dim(down_weight[0], wanted * (8 * units), 8 * units, 1)
        return lax.ppermute(block, "grp", moves(step, 0)) if step else block

    attn = spread(attn, NZ, "grp", GATHER)
    attn = spread(attn.reshape(-1, attn.shape[2]), parts, "grp", REDUCE)
    projected = project(attn.reshape(parts, NZ, -1, attn.shape[2]), out_weight.T)
    projected, down_weight = lax.optimization_barrier((projected, down_weight))
    projected = exchange(projected, ("pool", "tp"))
    projected, down1, down3 = lax.optimization_barrier((projected, down_block(1), down_block(3)))
    slot_rows = head_sum(projected, residual, select)
    slot_rows = exchange(slot_rows.reshape(experts, slot_cap, columns), ("pool", "tp"))
    slot_rows, up_weight = lax.optimization_barrier((slot_rows, up_weight))
    same = spread(slot_rows.reshape(slots, columns).T, NZ, "grp", GATHER)
    same, up1, up3 = lax.optimization_barrier((same, up_block(1), up_block(3)))
    before = lax.ppermute(same[: NZ // 2], "grp", turns(1))
    after = lax.ppermute(same[NZ // 2 :], "grp", turns(-1))
    gain = norm_gain.reshape(NX, NZ, PAIR, columns)
    gain = lax.dynamic_index_in_dim(gain, x_index, 0, keepdims=False)
    gain = [lax.dynamic_index_in_dim(gain, m, 1, keepdims=False).reshape(-1) for m in (member, 1 - member)]
    gain = jnp.stack(gain)
    place = jnp.stack([x_index, member]).astype(jnp.int32)
    partial_up = up_product(place, (same, before, after), gain, (up_block(0), up1, up_block(2), up3))
    total_up = jnp.sum(exchange(partial_up, "grp", CROSS).astype(F32), axis=0)
    count = slots // units
    squares = (total_up[slots : slots + count] + total_up[slots + count : slots + 2 * count]).reshape(slots, 1)
    scale = lax.rsqrt(squares / width + 1e-06)
    act = jax.nn.silu(total_up[:slots] * scale).astype(BF16)

    act, down_weight = lax.optimization_barrier((act, down_weight))
    act = spread(act, 8, "grp", LINE)
    partial_out = exchange(down_product(place, act, (down_block(0), down1, down_block(2), down3)), "grp", CROSS)
    expert_out = jnp.sum(partial_out.astype(F32), axis=0).astype(BF16).T
    returned = exchange(expert_out.reshape(experts, slot_cap, columns), ("pool", "tp"))
    returned = returned.reshape(slots, columns)
    high = lax.reduce_precision(combine, 8, 7)
    dims = (((0,), (0,)), ((), ()))
    result = lax.dot_general(high.astype(BF16), returned, dims, preferred_element_type=F32)
    result += lax.dot_general((combine - high).astype(BF16), returned, dims, preferred_element_type=F32)
    return result.astype(BF16)


def solution(mesh):
    placed = (
        P("grp", ("pool", "tp")),
        P("grp", None, None),
        P("grp", None, None),
        P("grp"),
        P(("pool", "tp"), "grp"),
        P(("pool", "tp"), "grp"),
        P(),
        P(),
        P(),
        P(("pool", "tp"), None, "grp"),
        P(("pool", "tp"), "grp", None),
    )
    return jax.shard_map(
        shards, mesh=mesh, in_specs=placed, out_specs=P(("pool", "tp"), "grp"), check_vma=False
    )
```

```python
import jax
import jax.numpy as jnp
from jax import lax
from jax.experimental import pallas as pl
from jax.experimental.pallas import tpu as pltpu
from jax.sharding import PartitionSpec as P

BF16 = jnp.bfloat16
F32 = jnp.float32
NX, NZ, PAIR = 4, 4, 2
GATHER = [[x * 8 + z * 2 + m for z in range(NZ)] for x in range(NX) for m in range(PAIR)]
LINE = [[x * 8 + z for z in range(8)] for x in range(NX)]
CROSS = [[x * 8 + z for x in range(NX)] for z in range(8)]
REDUCE = [[x * 8 + z * 2 + m for x in range(NX) for m in range(PAIR)] for z in range(NZ)]


def moves(by_x, by_member):
    return [
        (x * 8 + z * 2 + m, (x + by_x) % NX * 8 + z * 2 + (m + by_member) % PAIR)
        for x in range(NX)
        for z in range(NZ)
        for m in range(PAIR)
    ]


def turns(by):
    return [(x * 8 + z, x * 8 + (z + by) % 8) for x in range(NX) for z in range(8)]


def spread(value, count, axis, groups=None):
    sent = jnp.broadcast_to(value[None], (count,) + value.shape)
    return lax.all_to_all(sent, axis, 0, 0, tiled=True, axis_index_groups=groups)


def exchange(value, axis, groups=None):
    return lax.all_to_all(value, axis, 0, 0, tiled=True, axis_index_groups=groups)


def whole(count):
    return [pl.BlockSpec(memory_space=pltpu.VMEM)] * count


PARAMS = pltpu.CompilerParams(vmem_limit_bytes=40 * 2**20)


def project_kernel(attn, weight, out):
    run = attn.shape[2]
    dims = (((1,), (1,)), ((), ()))
    for x in range(NX):
        value = jnp.concatenate(
            [attn[x * PAIR + m].reshape(NZ * run, attn.shape[3]) for m in range(PAIR)], axis=0
        )
        value = lax.dot_general(value, weight[...], dims, preferred_element_type=F32).astype(BF16)
        for m in range(PAIR):
            for z in range(NZ):
                first = (m * NZ + z) * run
                out[x * NZ + z, m * run : (m + 1) * run] = value[first : first + run]


def project(attn, weight):
    rows, columns = PAIR * attn.shape[2], weight.shape[0]
    return pl.pallas_call(
        project_kernel,
        out_shape=jax.ShapeDtypeStruct((NX * NZ, rows, columns), BF16),
        in_specs=whole(2),
        out_specs=whole(1)[0],
        compiler_params=PARAMS,
        cost_estimate=pl.CostEstimate(
            flops=2 * NX * NZ * rows * columns * weight.shape[1], bytes_accessed=2 * 2**20, transcendentals=0
        ),
    )(attn, weight)


def head_sum_kernel(parts, residual, select, out):
    total = residual[...].astype(F32)
    for i in range(parts.shape[0]):
        total += parts[i].astype(F32)
    out[...] = jnp.dot(select[...], total.astype(BF16), preferred_element_type=F32).astype(BF16)


def head_sum(parts, residual, select):
    slots, columns = select.shape[0], residual.shape[1]
    return pl.pallas_call(
        head_sum_kernel,
        out_shape=jax.ShapeDtypeStruct((slots, columns), BF16),
        in_specs=whole(3),
        out_specs=whole(1)[0],
        compiler_params=PARAMS,
        cost_estimate=pl.CostEstimate(
            flops=2 * slots * columns * residual.shape[0], bytes_accessed=2**20, transcendentals=0
        ),
    )(parts, residual, select)


def up_kernel(place, same, before, after, gain, block0, block1, block2, block3, out):
    x_index, member = place[0], place[1]
    slots, units = same.shape[2], out.shape[2]
    depth = NZ * same.shape[1]
    other = jnp.concatenate([r[...].reshape(depth // 2, slots) for r in (before, after)], axis=0)
    normed, squares = [], 0.0
    for i, value in enumerate((same[...].reshape(depth, slots), other)):
        squares += jnp.sum(jnp.square(value.astype(F32)), axis=0, keepdims=True)
        normed.append((value.T.astype(F32) * gain[i : i + 1, :]).astype(BF16))
    row = lax.broadcasted_iota(jnp.int32, (16, units), 0)
    count = slots // units
    tail = jnp.zeros((16, units), F32)
    for i in range(count):
        part = jnp.broadcast_to(squares[:, i * units : (i + 1) * units], (16, units))
        high = part.astype(BF16).astype(F32)
        tail = jnp.where(row == i, high, tail)
        tail = jnp.where(row == count + i, part - high, tail)
    tail = tail.astype(BF16)
    for step, block in ((0, (block0, block1)), (2, (block2, block3))):
        total = 0.0
        for value, which in zip(normed, (member, 1 - member)):
            weight = jnp.concatenate([b[:, which].reshape(depth, units) for b in block], axis=1)
            total += jnp.dot(value, weight, preferred_element_type=F32)
        total = total.astype(BF16)
        for i in range(2):
            target = lax.rem(x_index + NX - step - i, NX)
            out[target, :slots] = total[:, i * units : (i + 1) * units]
            out[target, slots:] = tail


def up_product(place, rows, gain, blocks):
    count, columns, slots = rows[0].shape
    units = blocks[0].shape[3]
    return pl.pallas_call(
        up_kernel,
        out_shape=jax.ShapeDtypeStruct((NX, slots + 16, units), BF16),
        in_specs=[pl.BlockSpec(memory_space=pltpu.SMEM)] + whole(8),
        out_specs=whole(1)[0],
        compiler_params=PARAMS,
        cost_estimate=pl.CostEstimate(
            flops=4 * slots * columns * count * NX * units, bytes_accessed=6 * 2**20, transcendentals=0
        ),
    )(place, *rows, gain, *blocks)


def down_kernel(place, act, block0, block1, block2, block3, out):
    x_index = place[0]
    count, units = act.shape[0], act.shape[2]
    dims = (((1,), (1,)), ((), ()))
    joined = [jnp.concatenate([act[z], act[z + 1]], axis=1) for z in range(0, count, 2)]
    for step, block in enumerate((block0, block1, block2, block3)):
        total = 0.0
        for z in range(count // 2):
            weight = block[:, 2 * z * units : 2 * (z + 1) * units]
            total += lax.dot_general(weight, joined[z], dims, preferred_element_type=F32)
        out[lax.rem(x_index + NX - step, NX)] = total.astype(BF16)


def down_product(place, act, blocks):
    count, slots, units = act.shape
    columns = blocks[0].shape[0]
    return pl.pallas_call(
        down_kernel,
        out_shape=jax.ShapeDtypeStruct((NX, columns, slots), BF16),
        in_specs=[pl.BlockSpec(memory_space=pltpu.SMEM)] + whole(5),
        out_specs=whole(1)[0],
        compiler_params=PARAMS,
        cost_estimate=pl.CostEstimate(
            flops=2 * slots * columns * NX * count * units, bytes_accessed=5 * 2**20, transcendentals=0
        ),
    )(place, act, *blocks)


def attend(queries, keys, values, lengths):
    group_rows, ctx_len, head_size = keys.shape
    query_heads = queries.reshape(group_rows, -1, head_size)
    scores = jnp.einsum("rhd,rjd->rhj", query_heads, keys, preferred_element_type=F32)
    scores = scores * head_size ** (-0.5)
    valid = jnp.arange(ctx_len, dtype=jnp.int32)[None, None, :] < lengths[:, None, None]
    scores = jnp.where(valid, scores, -1e30)
    highest = jnp.max(scores, axis=-1, keepdims=True)
    weights = jnp.exp(scores - highest)
    probs = (weights / jnp.sum(weights, axis=-1, keepdims=True)).astype(BF16)
    attn = jnp.einsum("rhj,rjd->rhd", probs, values, preferred_element_type=F32)
    return attn.astype(BF16).reshape(queries.shape)


def shards(
    queries,
    keys,
    values,
    lengths,
    out_weight,
    residual,
    norm_gain,
    routes,
    route_weight,
    up_weight,
    down_weight,
):
    experts = lax.axis_size(("pool", "tp"))
    block_index = lax.axis_index(("pool", "tp"))
    group_index = lax.axis_index("grp")
    x_index, member = group_index // (NZ * PAIR), group_index % PAIR
    rows, columns = residual.shape
    top_count = routes.shape[1]
    slot_cap = min(rows, rows * top_count * 2 // experts)
    slots = experts * slot_cap
    width = norm_gain.shape[0]
    units = up_weight.shape[2]
    parts = NX * PAIR

    own_routes = lax.dynamic_slice_in_dim(routes, block_index * rows, rows, 0)
    own_weight = lax.dynamic_slice_in_dim(route_weight, block_index * rows, rows, 0)
    named = own_routes.T[:, None, :] == jnp.arange(experts, dtype=jnp.int32)[None, :, None]
    weight_of = jnp.sum(jnp.where(named, own_weight.T[:, None, :], 0.0), axis=0)
    named = jnp.any(named, axis=0)
    earlier = jnp.arange(rows)[:, None] < jnp.arange(rows)[None, :]
    place = jnp.dot(named.astype(BF16), earlier.astype(BF16), preferred_element_type=F32)
    here = place.astype(jnp.int32)[:, None, :] == jnp.arange(slot_cap, dtype=jnp.int32)[None, :, None]
    here = jnp.logical_and(here, named[:, None, :])
    select = here.astype(BF16).reshape(slots, rows)
    combine = jnp.where(here, weight_of[:, None, :], 0.0).reshape(slots, rows)

    attn = attend(queries, keys, values, lengths)
    def up_block(step):
        wanted = (x_index + step) % NX
        block = lax.dynamic_slice_in_dim(up_weight[0], wanted * (width // NX), width // NX, 0)
        block = lax.ppermute(block, "grp", moves(step, 0)) if step else block
        return block.reshape(NZ, PAIR, columns, units)

    def down_block(step):
        wanted = (x_index + step) % NX
        block = lax.dynamic_slice_in_dim(down_weight[0], wanted * (8 * units), 8 * units, 1)
        return lax.ppermute(block, "grp", moves(step, 0)) if step else block

    attn = spread(attn, NZ, "grp", GATHER)
    attn = spread(attn.reshape(-1, attn.shape[2]), parts, "grp", REDUCE)
    projected = project(attn.reshape(parts, NZ, -1, attn.shape[2]), out_weight.T)
    projected, up_weight = lax.optimization_barrier((projected, up_weight))
    projected = exchange(projected, ("pool", "tp"))
    projected, up1, up3 = lax.optimization_barrier((projected, up_block(1), up_block(3)))
    slot_rows = head_sum(projected, residual, select)
    slot_rows = exchange(slot_rows.reshape(experts, slot_cap, columns), ("pool", "tp"))
    slot_rows, up_weight, down_weight = lax.optimization_barrier((slot_rows, up_weight, down_weight))
    same = spread(slot_rows.reshape(slots, columns).T, NZ, "grp", GATHER)
    before = lax.ppermute(same[: NZ // 2], "grp", turns(1))
    after = lax.ppermute(same[NZ // 2 :], "grp", turns(-1))
    before, after, down1, down3 = lax.optimization_barrier((before, after, down_block(1), down_block(3)))
    gain = norm_gain.reshape(NX, NZ, PAIR, columns)
    gain = lax.dynamic_index_in_dim(gain, x_index, 0, keepdims=False)
    gain = [lax.dynamic_index_in_dim(gain, m, 1, keepdims=False).reshape(-1) for m in (member, 1 - member)]
    gain = jnp.stack(gain)
    place = jnp.stack([x_index, member]).astype(jnp.int32)
    partial_up = up_product(place, (same, before, after), gain, (up_block(0), up1, up_block(2), up3))
    total_up = jnp.sum(exchange(partial_up, "grp", CROSS).astype(F32), axis=0)
    count = slots // units
    squares = (total_up[slots : slots + count] + total_up[slots + count : slots + 2 * count]).reshape(slots, 1)
    scale = lax.rsqrt(squares / width + 1e-06)
    act = jax.nn.silu(total_up[:slots] * scale).astype(BF16)

    act, down_weight = lax.optimization_barrier((act, down_weight))
    act = spread(act, 8, "grp", LINE)
    partial_out = exchange(down_product(place, act, (down_block(0), down1, down_block(2), down3)), "grp", CROSS)
    expert_out = jnp.sum(partial_out.astype(F32), axis=0).astype(BF16).T
    returned = exchange(expert_out.reshape(experts, slot_cap, columns), ("pool", "tp"))
    returned = returned.reshape(slots, columns)
    high = lax.reduce_precision(combine, 8, 7)
    dims = (((0,), (0,)), ((), ()))
    result = lax.dot_general(high.astype(BF16), returned, dims, preferred_element_type=F32)
    result += lax.dot_general((combine - high).astype(BF16), returned, dims, preferred_element_type=F32)
    return result.astype(BF16)


def solution(mesh):
    placed = (
        P("grp", ("pool", "tp")),
        P("grp", None, None),
        P("grp", None, None),
        P("grp"),
        P(("pool", "tp"), "grp"),
        P(("pool", "tp"), "grp"),
        P(),
        P(),
        P(),
        P(("pool", "tp"), None, "grp"),
        P(("pool", "tp"), "grp", None),
    )
    return jax.shard_map(
        shards, mesh=mesh, in_specs=placed, out_specs=P(("pool", "tp"), "grp"), check_vma=False
    )
```

```python
import jax
import jax.numpy as jnp
from jax import lax
from jax.experimental import pallas as pl
from jax.experimental.pallas import tpu as pltpu
from jax.sharding import Mesh
from jax.sharding import PartitionSpec as P

BF16 = jnp.bfloat16
F32 = jnp.float32
NX, NZ, PAIR = 4, 4, 2
GRP = ("x", "zpair", "member")


def moves(by_x, by_member):
    return [
        (x * 8 + z * 2 + m, (x + by_x) % NX * 8 + z * 2 + (m + by_member) % PAIR)
        for x in range(NX)
        for z in range(NZ)
        for m in range(PAIR)
    ]


def turns(by):
    return [(x * 8 + z, x * 8 + (z + by) % 8) for x in range(NX) for z in range(8)]


def exchange(value, axis):
    return lax.all_to_all(value, axis, 0, 0, tiled=True)


def spread(value, count, axis):
    return exchange(jnp.broadcast_to(value[None], (count,) + value.shape), axis)


def whole(count):
    return [pl.BlockSpec(memory_space=pltpu.VMEM)] * count


PARAMS = pltpu.CompilerParams(vmem_limit_bytes=40 * 2**20)


def project_kernel(attn, weight, out):
    run = attn.shape[2]
    dims = (((1,), (1,)), ((), ()))
    for x in range(NX):
        value = jnp.concatenate(
            [attn[x * PAIR + m].reshape(NZ * run, attn.shape[3]) for m in range(PAIR)], axis=0
        )
        value = lax.dot_general(value, weight[...], dims, preferred_element_type=F32).astype(BF16)
        for m in range(PAIR):
            for z in range(NZ):
                first = (m * NZ + z) * run
                out[x * NZ + z, m * run : (m + 1) * run] = value[first : first + run]


def project(attn, weight):
    rows, columns = PAIR * attn.shape[2], weight.shape[0]
    return pl.pallas_call(
        project_kernel,
        out_shape=jax.ShapeDtypeStruct((NX * NZ, rows, columns), BF16),
        in_specs=whole(2),
        out_specs=whole(1)[0],
        compiler_params=PARAMS,
        cost_estimate=pl.CostEstimate(
            flops=2 * NX * NZ * rows * columns * weight.shape[1], bytes_accessed=2 * 2**20, transcendentals=0
        ),
    )(attn, weight)


def head_sum_kernel(parts, residual, select, out):
    total = residual[...].astype(F32)
    for i in range(parts.shape[0]):
        total += parts[i].astype(F32)
    out[...] = jnp.dot(select[...], total.astype(BF16), preferred_element_type=F32).astype(BF16)


def head_sum(parts, residual, select):
    slots, columns = select.shape[0], residual.shape[1]
    return pl.pallas_call(
        head_sum_kernel,
        out_shape=jax.ShapeDtypeStruct((slots, columns), BF16),
        in_specs=whole(3),
        out_specs=whole(1)[0],
        compiler_params=PARAMS,
        cost_estimate=pl.CostEstimate(
            flops=2 * slots * columns * residual.shape[0], bytes_accessed=2**20, transcendentals=0
        ),
    )(parts, residual, select)


def up_kernel(place, same, before, after, gain, block0, block1, block2, block3, out):
    x_index, member = place[0], place[1]
    slots, units = same.shape[2], out.shape[2]
    depth = NZ * same.shape[1]
    other = jnp.concatenate([r[...].reshape(depth // 2, slots) for r in (before, after)], axis=0)
    normed, squares = [], 0.0
    for i, value in enumerate((same[...].reshape(depth, slots), other)):
        squares += jnp.sum(jnp.square(value.astype(F32)), axis=0, keepdims=True)
        normed.append((value.T.astype(F32) * gain[i : i + 1, :]).astype(BF16))
    row = lax.broadcasted_iota(jnp.int32, (16, units), 0)
    count = slots // units
    tail = jnp.zeros((16, units), F32)
    for i in range(count):
        part = jnp.broadcast_to(squares[:, i * units : (i + 1) * units], (16, units))
        high = part.astype(BF16).astype(F32)
        tail = jnp.where(row == i, high, tail)
        tail = jnp.where(row == count + i, part - high, tail)
    tail = tail.astype(BF16)
    for step, block in ((0, (block0, block1)), (2, (block2, block3))):
        total = 0.0
        for value, which in zip(normed, (member, 1 - member)):
            weight = jnp.concatenate([b[:, which].reshape(depth, units) for b in block], axis=1)
            total += jnp.dot(value, weight, preferred_element_type=F32)
        total = total.astype(BF16)
        for i in range(2):
            target = lax.rem(x_index + NX - step - i, NX)
            out[target, :slots] = total[:, i * units : (i + 1) * units]
            out[target, slots:] = tail


def up_product(place, rows, gain, blocks):
    count, columns, slots = rows[0].shape
    units = blocks[0].shape[3]
    return pl.pallas_call(
        up_kernel,
        out_shape=jax.ShapeDtypeStruct((NX, slots + 16, units), BF16),
        in_specs=[pl.BlockSpec(memory_space=pltpu.SMEM)] + whole(8),
        out_specs=whole(1)[0],
        compiler_params=PARAMS,
        cost_estimate=pl.CostEstimate(
            flops=4 * slots * columns * count * NX * units, bytes_accessed=6 * 2**20, transcendentals=0
        ),
    )(place, *rows, gain, *blocks)


def down_kernel(place, act, block0, block1, block2, block3, out):
    x_index = place[0]
    count, units = act.shape[0], act.shape[2]
    dims = (((1,), (1,)), ((), ()))
    joined = [jnp.concatenate([act[z], act[z + 1]], axis=1) for z in range(0, count, 2)]
    for step, block in enumerate((block0, block1, block2, block3)):
        total = 0.0
        for z in range(count // 2):
            weight = block[:, 2 * z * units : 2 * (z + 1) * units]
            total += lax.dot_general(weight, joined[z], dims, preferred_element_type=F32)
        out[lax.rem(x_index + NX - step, NX)] = total.astype(BF16)


def down_product(place, act, blocks):
    count, slots, units = act.shape
    columns = blocks[0].shape[0]
    return pl.pallas_call(
        down_kernel,
        out_shape=jax.ShapeDtypeStruct((NX, columns, slots), BF16),
        in_specs=[pl.BlockSpec(memory_space=pltpu.SMEM)] + whole(5),
        out_specs=whole(1)[0],
        compiler_params=PARAMS,
        cost_estimate=pl.CostEstimate(
            flops=2 * slots * columns * NX * count * units, bytes_accessed=5 * 2**20, transcendentals=0
        ),
    )(place, act, *blocks)


def attend(queries, keys, values, lengths):
    group_rows, ctx_len, head_size = keys.shape
    query_heads = queries.reshape(group_rows, -1, head_size)
    scores = jnp.einsum("rhd,rjd->rhj", query_heads, keys, preferred_element_type=F32)
    scores = scores * head_size ** (-0.5)
    valid = jnp.arange(ctx_len, dtype=jnp.int32)[None, None, :] < lengths[:, None, None]
    scores = jnp.where(valid, scores, -1e30)
    highest = jnp.max(scores, axis=-1, keepdims=True)
    weights = jnp.exp(scores - highest)
    probs = (weights / jnp.sum(weights, axis=-1, keepdims=True)).astype(BF16)
    attn = jnp.einsum("rhj,rjd->rhd", probs, values, preferred_element_type=F32)
    return attn.astype(BF16).reshape(queries.shape)


def shards(
    queries,
    keys,
    values,
    lengths,
    out_weight,
    residual,
    norm_gain,
    routes,
    route_weight,
    up_weight,
    down_weight,
):
    experts = lax.axis_size(("pool", "tp"))
    block_index = lax.axis_index(("pool", "tp"))
    group_index = lax.axis_index(GRP)
    x_index, member = group_index // (NZ * PAIR), group_index % PAIR
    rows, columns = residual.shape
    top_count = routes.shape[1]
    slot_cap = min(rows, rows * top_count * 2 // experts)
    slots = experts * slot_cap
    width = norm_gain.shape[0]
    units = up_weight.shape[2]
    parts = NX * PAIR

    own_routes = lax.dynamic_slice_in_dim(routes, block_index * rows, rows, 0)
    own_weight = lax.dynamic_slice_in_dim(route_weight, block_index * rows, rows, 0)
    named = own_routes.T[:, None, :] == jnp.arange(experts, dtype=jnp.int32)[None, :, None]
    weight_of = jnp.sum(jnp.where(named, own_weight.T[:, None, :], 0.0), axis=0)
    named = jnp.any(named, axis=0)
    earlier = jnp.arange(rows)[:, None] < jnp.arange(rows)[None, :]
    place = jnp.dot(named.astype(BF16), earlier.astype(BF16), preferred_element_type=F32)
    here = place.astype(jnp.int32)[:, None, :] == jnp.arange(slot_cap, dtype=jnp.int32)[None, :, None]
    here = jnp.logical_and(here, named[:, None, :])
    select = here.astype(BF16).reshape(slots, rows)
    combine = jnp.where(here, weight_of[:, None, :], 0.0).reshape(slots, rows)

    attn = attend(queries, keys, values, lengths)
    def up_block(step):
        wanted = (x_index + step) % NX
        block = lax.dynamic_slice_in_dim(up_weight[0], wanted * (width // NX), width // NX, 0)
        block = lax.ppermute(block, GRP, moves(step, 0)) if step else block
        return block.reshape(NZ, PAIR, columns, units)

    def down_block(step):
        wanted = (x_index + step) % NX
        block = lax.dynamic_slice_in_dim(down_weight[0], wanted * (8 * units), 8 * units, 1)
        return lax.ppermute(block, GRP, moves(step, 0)) if step else block

    attn = spread(attn, NZ, "zpair")
    attn = spread(attn.reshape(-1, attn.shape[2]), parts, ("x", "member"))
    projected = project(attn.reshape(parts, NZ, -1, attn.shape[2]), out_weight.T)
    projected, up_weight = lax.optimization_barrier((projected, up_weight))
    projected = exchange(projected, ("pool", "tp"))
    projected, up1, up3 = lax.optimization_barrier((projected, up_block(1), up_block(3)))
    slot_rows = head_sum(projected, residual, select)
    slot_rows, up_weight, down_weight = lax.optimization_barrier((slot_rows, up_weight, down_weight))
    same = jnp.broadcast_to(slot_rows.reshape(experts, 1, slot_cap, columns), (experts, NZ, slot_cap, columns))
    same = exchange(same.reshape(experts * NZ, slot_cap, columns), ("pool", "tp", "zpair"))
    same = same.reshape(experts, NZ, slot_cap, columns).transpose(1, 3, 0, 2).reshape(NZ, columns, slots)
    before = lax.ppermute(same[: NZ // 2], GRP, turns(1))
    after = lax.ppermute(same[NZ // 2 :], GRP, turns(-1))
    before, after, down1, down3 = lax.optimization_barrier((before, after, down_block(1), down_block(3)))
    gain = norm_gain.reshape(NX, NZ, PAIR, columns)
    gain = lax.dynamic_index_in_dim(gain, x_index, 0, keepdims=False)
    gain = [lax.dynamic_index_in_dim(gain, m, 1, keepdims=False).reshape(-1) for m in (member, 1 - member)]
    gain = jnp.stack(gain)
    place = jnp.stack([x_index, member]).astype(jnp.int32)
    partial_up = up_product(place, (same, before, after), gain, (up_block(0), up1, up_block(2), up3))
    total_up = jnp.sum(exchange(partial_up, "x").astype(F32), axis=0)
    count = slots // units
    squares = (total_up[slots : slots + count] + total_up[slots + count : slots + 2 * count]).reshape(slots, 1)
    scale = lax.rsqrt(squares / width + 1e-06)
    act = jax.nn.silu(total_up[:slots] * scale).astype(BF16)

    act, down_weight = lax.optimization_barrier((act, down_weight))
    act = spread(act, 8, ("zpair", "member"))
    partial_out = exchange(down_product(place, act, (down_block(0), down1, down_block(2), down3)), "x")
    expert_out = jnp.sum(partial_out.astype(F32), axis=0).astype(BF16).T
    returned = exchange(expert_out.reshape(experts, slot_cap, columns), ("pool", "tp"))
    returned = returned.reshape(slots, columns)
    high = lax.reduce_precision(combine, 8, 7)
    dims = (((0,), (0,)), ((), ()))
    result = lax.dot_general(high.astype(BF16), returned, dims, preferred_element_type=F32)
    result += lax.dot_general((combine - high).astype(BF16), returned, dims, preferred_element_type=F32)
    return result.astype(BF16)


def solution(mesh):
    devices = mesh.devices.reshape(2, NX, NZ, PAIR, 8)
    finer = Mesh(devices, ("pool",) + GRP + ("tp",), axis_types=(mesh.axis_types[0],) * 5)
    placed = (
        P(GRP, ("pool", "tp")),
        P(GRP, None, None),
        P(GRP, None, None),
        P(GRP),
        P(("pool", "tp"), GRP),
        P(("pool", "tp"), GRP),
        P(),
        P(),
        P(),
        P(("pool", "tp"), None, GRP),
        P(("pool", "tp"), GRP, None),
    )
    return jax.shard_map(
        shards, mesh=finer, in_specs=placed, out_specs=P(("pool", "tp"), GRP), check_vma=False
    )
```

```python
import jax
import jax.numpy as jnp
from jax import lax
from jax.experimental import pallas as pl
from jax.experimental.pallas import tpu as pltpu
from jax.sharding import Mesh
from jax.sharding import PartitionSpec as P

BF16 = jnp.bfloat16
F32 = jnp.float32
NX, NZ, PAIR = 4, 4, 2
GRP = ("x", "zpair", "member")


def moves(by_x, by_member):
    return [
        (x * 8 + z * 2 + m, (x + by_x) % NX * 8 + z * 2 + (m + by_member) % PAIR)
        for x in range(NX)
        for z in range(NZ)
        for m in range(PAIR)
    ]


def turns(by):
    return [(x * 8 + z, x * 8 + (z + by) % 8) for x in range(NX) for z in range(8)]


def exchange(value, axis):
    return lax.all_to_all(value, axis, 0, 0, tiled=True)


def spread(value, count, axis):
    return exchange(jnp.broadcast_to(value[None], (count,) + value.shape), axis)


def whole(count):
    return [pl.BlockSpec(memory_space=pltpu.VMEM)] * count


PARAMS = pltpu.CompilerParams(vmem_limit_bytes=40 * 2**20)


def project_kernel(attn, weight, out):
    run = attn.shape[2]
    dims = (((1,), (1,)), ((), ()))
    for x in range(NX):
        value = jnp.concatenate(
            [attn[x * PAIR + m].reshape(NZ * run, attn.shape[3]) for m in range(PAIR)], axis=0
        )
        value = lax.dot_general(value, weight[...], dims, preferred_element_type=F32).astype(BF16)
        for m in range(PAIR):
            for z in range(NZ):
                first = (m * NZ + z) * run
                out[x * NZ + z, m * run : (m + 1) * run] = value[first : first + run]


def project(attn, weight):
    rows, columns = PAIR * attn.shape[2], weight.shape[0]
    return pl.pallas_call(
        project_kernel,
        out_shape=jax.ShapeDtypeStruct((NX * NZ, rows, columns), BF16),
        in_specs=whole(2),
        out_specs=whole(1)[0],
        compiler_params=PARAMS,
        cost_estimate=pl.CostEstimate(
            flops=2 * NX * NZ * rows * columns * weight.shape[1], bytes_accessed=2 * 2**20, transcendentals=0
        ),
    )(attn, weight)


def head_sum_kernel(parts, residual, select, out):
    total = residual[...].astype(F32)
    for i in range(parts.shape[0]):
        total += parts[i].astype(F32)
    out[...] = jnp.dot(select[...], total.astype(BF16), preferred_element_type=F32).astype(BF16)


def head_sum(parts, residual, select):
    slots, columns = select.shape[0], residual.shape[1]
    return pl.pallas_call(
        head_sum_kernel,
        out_shape=jax.ShapeDtypeStruct((slots, columns), BF16),
        in_specs=whole(3),
        out_specs=whole(1)[0],
        compiler_params=PARAMS,
        cost_estimate=pl.CostEstimate(
            flops=2 * slots * columns * residual.shape[0], bytes_accessed=2**20, transcendentals=0
        ),
    )(parts, residual, select)


def up_kernel(place, same, before, after, gain, block0, block1, block2, block3, out):
    x_index, member = place[0], place[1]
    slots, units = same.shape[1], out.shape[2]
    ones = jnp.ones((16, same.shape[2]), BF16)
    dims = (((1,), (1,)), ((), ()))
    rows = [same[z] for z in range(NZ)] + [r[z] for r in (before, after) for z in range(NZ // 2)]
    normed, squares = [], 0.0
    for i, value in enumerate(rows):
        value = value.astype(F32)
        normed.append((value * gain[i : i + 1, :]).astype(BF16))
        square = value * value
        high = square.astype(BF16)
        low = (square - high.astype(F32)).astype(BF16)
        squares += lax.dot_general(ones, high, dims, preferred_element_type=F32)
        squares += lax.dot_general(ones, low, dims, preferred_element_type=F32)
    row = lax.broadcasted_iota(jnp.int32, (16, units), 0)
    count = slots // units
    tail = jnp.zeros((16, units), F32)
    for i in range(count):
        part = squares[:, i * units : (i + 1) * units]
        high = part.astype(BF16).astype(F32)
        tail = jnp.where(row == i, high, tail)
        tail = jnp.where(row == count + i, part - high, tail)
    tail = tail.astype(BF16)
    for step, block in ((0, (block0, block1)), (2, (block2, block3))):
        total = 0.0
        for i, value in enumerate(normed):
            which = member if i < NZ else 1 - member
            weight = jnp.concatenate([b[i % NZ, which] for b in block], axis=1)
            total += jnp.dot(value, weight, preferred_element_type=F32)
        total = total.astype(BF16)
        for i in range(2):
            target = lax.rem(x_index + NX - step - i, NX)
            out[target, :slots] = total[:, i * units : (i + 1) * units]
            out[target, slots:] = tail


def up_product(place, rows, gain, blocks):
    count, slots, columns = rows[0].shape
    units = blocks[0].shape[3]
    return pl.pallas_call(
        up_kernel,
        out_shape=jax.ShapeDtypeStruct((NX, slots + 16, units), BF16),
        in_specs=[pl.BlockSpec(memory_space=pltpu.SMEM)] + whole(8),
        out_specs=whole(1)[0],
        compiler_params=PARAMS,
        cost_estimate=pl.CostEstimate(
            flops=4 * slots * columns * count * NX * units, bytes_accessed=6 * 2**20, transcendentals=0
        ),
    )(place, *rows, gain, *blocks)


def down_kernel(place, act, block0, block1, block2, block3, out):
    x_index = place[0]
    count, units = act.shape[0], act.shape[2]
    dims = (((1,), (1,)), ((), ()))
    joined = [jnp.concatenate([act[z], act[z + 1]], axis=1) for z in range(0, count, 2)]
    for step, block in enumerate((block0, block1, block2, block3)):
        total = 0.0
        for z in range(count // 2):
            weight = block[:, 2 * z * units : 2 * (z + 1) * units]
            total += lax.dot_general(weight, joined[z], dims, preferred_element_type=F32)
        out[lax.rem(x_index + NX - step, NX)] = total.astype(BF16)


def down_product(place, act, blocks):
    count, slots, units = act.shape
    columns = blocks[0].shape[0]
    return pl.pallas_call(
        down_kernel,
        out_shape=jax.ShapeDtypeStruct((NX, columns, slots), BF16),
        in_specs=[pl.BlockSpec(memory_space=pltpu.SMEM)] + whole(5),
        out_specs=whole(1)[0],
        compiler_params=PARAMS,
        cost_estimate=pl.CostEstimate(
            flops=2 * slots * columns * NX * count * units, bytes_accessed=5 * 2**20, transcendentals=0
        ),
    )(place, act, *blocks)


def attend(queries, keys, values, lengths):
    group_rows, ctx_len, head_size = keys.shape
    query_heads = queries.reshape(group_rows, -1, head_size)
    scores = jnp.einsum("rhd,rjd->rhj", query_heads, keys, preferred_element_type=F32)
    scores = scores * head_size ** (-0.5)
    valid = jnp.arange(ctx_len, dtype=jnp.int32)[None, None, :] < lengths[:, None, None]
    scores = jnp.where(valid, scores, -1e30)
    highest = jnp.max(scores, axis=-1, keepdims=True)
    weights = jnp.exp(scores - highest)
    probs = (weights / jnp.sum(weights, axis=-1, keepdims=True)).astype(BF16)
    attn = jnp.einsum("rhj,rjd->rhd", probs, values, preferred_element_type=F32)
    return attn.astype(BF16).reshape(queries.shape)


def shards(
    queries,
    keys,
    values,
    lengths,
    out_weight,
    residual,
    norm_gain,
    routes,
    route_weight,
    up_weight,
    down_weight,
):
    experts = lax.axis_size(("pool", "tp"))
    block_index = lax.axis_index(("pool", "tp"))
    group_index = lax.axis_index(GRP)
    x_index, member = group_index // (NZ * PAIR), group_index % PAIR
    rows, columns = residual.shape
    top_count = routes.shape[1]
    slot_cap = min(rows, rows * top_count * 2 // experts)
    slots = experts * slot_cap
    width = norm_gain.shape[0]
    units = up_weight.shape[2]
    parts = NX * PAIR

    own_routes = lax.dynamic_slice_in_dim(routes, block_index * rows, rows, 0)
    own_weight = lax.dynamic_slice_in_dim(route_weight, block_index * rows, rows, 0)
    named = own_routes.T[:, None, :] == jnp.arange(experts, dtype=jnp.int32)[None, :, None]
    weight_of = jnp.sum(jnp.where(named, own_weight.T[:, None, :], 0.0), axis=0)
    named = jnp.any(named, axis=0)
    earlier = jnp.arange(rows)[:, None] < jnp.arange(rows)[None, :]
    place = jnp.dot(named.astype(BF16), earlier.astype(BF16), preferred_element_type=F32)
    here = place.astype(jnp.int32)[:, None, :] == jnp.arange(slot_cap, dtype=jnp.int32)[None, :, None]
    here = jnp.logical_and(here, named[:, None, :])
    select = here.astype(BF16).reshape(slots, rows)
    combine = jnp.where(here, weight_of[:, None, :], 0.0).reshape(slots, rows)

    attn = attend(queries, keys, values, lengths)
    def up_block(step):
        wanted = (x_index + step) % NX
        block = lax.dynamic_slice_in_dim(up_weight[0], wanted * (width // NX), width // NX, 0)
        block = lax.ppermute(block, GRP, moves(step, 0)) if step else block
        return block.reshape(NZ, PAIR, columns, units)

    def down_block(step):
        wanted = (x_index + step) % NX
        block = lax.dynamic_slice_in_dim(down_weight[0], wanted * (8 * units), 8 * units, 1)
        return lax.ppermute(block, GRP, moves(step, 0)) if step else block

    attn = spread(attn, NZ, "zpair")
    attn = spread(attn.reshape(-1, attn.shape[2]), parts, ("x", "member"))
    projected = project(attn.reshape(parts, NZ, -1, attn.shape[2]), out_weight.T)
    projected, up_weight = lax.optimization_barrier((projected, up_weight))
    projected = exchange(projected, ("pool", "tp"))
    projected, up1, up3 = lax.optimization_barrier((projected, up_block(1), up_block(3)))
    slot_rows = head_sum(projected, residual, select)
    slot_rows, up_weight, down_weight = lax.optimization_barrier((slot_rows, up_weight, down_weight))
    same = jnp.broadcast_to(slot_rows.reshape(1, experts, slot_cap, columns), (NZ, experts, slot_cap, columns))
    same = exchange(same.reshape(NZ * experts, slot_cap, columns), ("zpair", "pool", "tp"))
    same = same.reshape(NZ, slots, columns)
    before = lax.ppermute(same[: NZ // 2], GRP, turns(1))
    after = lax.ppermute(same[NZ // 2 :], GRP, turns(-1))
    before, after, down1, down3 = lax.optimization_barrier((before, after, down_block(1), down_block(3)))
    gain = norm_gain.reshape(NX, NZ, PAIR, columns)
    gain = lax.dynamic_index_in_dim(gain, x_index, 0, keepdims=False)
    gain = [lax.dynamic_index_in_dim(gain, m, 1, keepdims=False) for m in (member, 1 - member)]
    gain = jnp.concatenate(gain)
    place = jnp.stack([x_index, member]).astype(jnp.int32)
    partial_up = up_product(place, (same, before, after), gain, (up_block(0), up1, up_block(2), up3))
    total_up = jnp.sum(exchange(partial_up, "x").astype(F32), axis=0)
    count = slots // units
    squares = (total_up[slots : slots + count] + total_up[slots + count : slots + 2 * count]).reshape(slots, 1)
    scale = lax.rsqrt(squares / width + 1e-06)
    act = jax.nn.silu(total_up[:slots] * scale).astype(BF16)

    act, down_weight = lax.optimization_barrier((act, down_weight))
    act = spread(act, 8, ("zpair", "member"))
    partial_out = exchange(down_product(place, act, (down_block(0), down1, down_block(2), down3)), "x")
    expert_out = jnp.sum(partial_out.astype(F32), axis=0).astype(BF16).T
    returned = exchange(expert_out.reshape(experts, slot_cap, columns), ("pool", "tp"))
    returned = returned.reshape(slots, columns)
    high = lax.reduce_precision(combine, 8, 7)
    dims = (((0,), (0,)), ((), ()))
    result = lax.dot_general(high.astype(BF16), returned, dims, preferred_element_type=F32)
    result += lax.dot_general((combine - high).astype(BF16), returned, dims, preferred_element_type=F32)
    return result.astype(BF16)


def solution(mesh):
    devices = mesh.devices.reshape(2, NX, NZ, PAIR, 8)
    finer = Mesh(devices, ("pool",) + GRP + ("tp",), axis_types=(mesh.axis_types[0],) * 5)
    placed = (
        P(GRP, ("pool", "tp")),
        P(GRP, None, None),
        P(GRP, None, None),
        P(GRP),
        P(("pool", "tp"), GRP),
        P(("pool", "tp"), GRP),
        P(),
        P(),
        P(),
        P(("pool", "tp"), None, GRP),
        P(("pool", "tp"), GRP, None),
    )
    return jax.shard_map(
        shards, mesh=finer, in_specs=placed, out_specs=P(("pool", "tp"), GRP), check_vma=False
    )
```

```python
import jax
import jax.numpy as jnp
from jax import lax
from jax.experimental import pallas as pl
from jax.experimental.pallas import tpu as pltpu
from jax.sharding import Mesh
from jax.sharding import PartitionSpec as P

BF16 = jnp.bfloat16
F32 = jnp.float32
NX, NZ, PAIR = 4, 4, 2
GRP = ("x", "zpair", "member")


def moves(by_x, by_member):
    return [
        (x * 8 + z * 2 + m, (x + by_x) % NX * 8 + z * 2 + (m + by_member) % PAIR)
        for x in range(NX)
        for z in range(NZ)
        for m in range(PAIR)
    ]


def turns(by):
    return [(x * 8 + z, x * 8 + (z + by) % 8) for x in range(NX) for z in range(8)]


def exchange(value, axis):
    return lax.all_to_all(value, axis, 0, 0, tiled=True)


def spread(value, count, axis):
    return exchange(jnp.broadcast_to(value[None], (count,) + value.shape), axis)


def whole(count):
    return [pl.BlockSpec(memory_space=pltpu.VMEM)] * count


PARAMS = pltpu.CompilerParams(vmem_limit_bytes=40 * 2**20)


def project_kernel(attn, weight, out):
    run = attn.shape[2]
    dims = (((1,), (1,)), ((), ()))
    for x in range(NX):
        value = jnp.concatenate(
            [attn[x * PAIR + m].reshape(NZ * run, attn.shape[3]) for m in range(PAIR)], axis=0
        )
        value = lax.dot_general(value, weight[...], dims, preferred_element_type=F32).astype(BF16)
        for m in range(PAIR):
            for z in range(NZ):
                first = (m * NZ + z) * run
                out[x * NZ + z, m * run : (m + 1) * run] = value[first : first + run]


def project(attn, weight):
    rows, columns = PAIR * attn.shape[2], weight.shape[0]
    return pl.pallas_call(
        project_kernel,
        out_shape=jax.ShapeDtypeStruct((NX * NZ, rows, columns), BF16),
        in_specs=whole(2),
        out_specs=whole(1)[0],
        compiler_params=PARAMS,
        cost_estimate=pl.CostEstimate(
            flops=2 * NX * NZ * rows * columns * weight.shape[1], bytes_accessed=2 * 2**20, transcendentals=0
        ),
    )(attn, weight)


def head_sum_kernel(parts, residual, select, out):
    total = residual[...].astype(F32)
    for i in range(parts.shape[0]):
        total += parts[i].astype(F32)
    value = jnp.dot(select[...], total.astype(BF16), preferred_element_type=F32).astype(BF16)
    for z in range(NZ):
        out[z] = value


def head_sum(parts, residual, select):
    slots, columns = select.shape[0], residual.shape[1]
    return pl.pallas_call(
        head_sum_kernel,
        out_shape=jax.ShapeDtypeStruct((NZ, slots, columns), BF16),
        in_specs=whole(3),
        out_specs=whole(1)[0],
        compiler_params=PARAMS,
        cost_estimate=pl.CostEstimate(
            flops=2 * slots * columns * residual.shape[0], bytes_accessed=2**20, transcendentals=0
        ),
    )(parts, residual, select)


def up_kernel(place, same, before, after, gain, block0, block1, block2, block3, out):
    x_index, member = place[0], place[1]
    slots, units = same.shape[1], out.shape[2]
    ones = jnp.ones((16, same.shape[2]), BF16)
    dims = (((1,), (1,)), ((), ()))
    rows = [same[z] for z in range(NZ)] + [r[z] for r in (before, after) for z in range(NZ // 2)]
    normed, squares = [], 0.0
    for i, value in enumerate(rows):
        value = value.astype(F32)
        normed.append((value * gain[i : i + 1, :]).astype(BF16))
        square = value * value
        high = square.astype(BF16)
        low = (square - high.astype(F32)).astype(BF16)
        squares += lax.dot_general(ones, high, dims, preferred_element_type=F32)
        squares += lax.dot_general(ones, low, dims, preferred_element_type=F32)
    row = lax.broadcasted_iota(jnp.int32, (16, units), 0)
    count = slots // units
    tail = jnp.zeros((16, units), F32)
    for i in range(count):
        part = squares[:, i * units : (i + 1) * units]
        high = part.astype(BF16).astype(F32)
        tail = jnp.where(row == i, high, tail)
        tail = jnp.where(row == count + i, part - high, tail)
    tail = tail.astype(BF16)
    for step, block in ((0, (block0, block1)), (2, (block2, block3))):
        total = 0.0
        for i, value in enumerate(normed):
            which = member if i < NZ else 1 - member
            weight = jnp.concatenate([b[i % NZ, which] for b in block], axis=1)
            total += jnp.dot(value, weight, preferred_element_type=F32)
        total = total.astype(BF16)
        for i in range(2):
            target = lax.rem(x_index + NX - step - i, NX)
            out[target, :slots] = total[:, i * units : (i + 1) * units]
            out[target, slots:] = tail


def up_product(place, rows, gain, blocks):
    count, slots, columns = rows[0].shape
    units = blocks[0].shape[3]
    return pl.pallas_call(
        up_kernel,
        out_shape=jax.ShapeDtypeStruct((NX, slots + 16, units), BF16),
        in_specs=[pl.BlockSpec(memory_space=pltpu.SMEM)] + whole(8),
        out_specs=whole(1)[0],
        compiler_params=PARAMS,
        cost_estimate=pl.CostEstimate(
            flops=4 * slots * columns * count * NX * units, bytes_accessed=6 * 2**20, transcendentals=0
        ),
    )(place, *rows, gain, *blocks)


def down_kernel(place, act, block0, block1, block2, block3, out):
    x_index = place[0]
    count, units = act.shape[0], act.shape[2]
    dims = (((1,), (1,)), ((), ()))
    joined = [jnp.concatenate([act[z], act[z + 1]], axis=1) for z in range(0, count, 2)]
    for step, block in enumerate((block0, block1, block2, block3)):
        total = 0.0
        for z in range(count // 2):
            weight = block[:, 2 * z * units : 2 * (z + 1) * units]
            total += lax.dot_general(weight, joined[z], dims, preferred_element_type=F32)
        out[lax.rem(x_index + NX - step, NX)] = total.astype(BF16)


def down_product(place, act, blocks):
    count, slots, units = act.shape
    columns = blocks[0].shape[0]
    return pl.pallas_call(
        down_kernel,
        out_shape=jax.ShapeDtypeStruct((NX, columns, slots), BF16),
        in_specs=[pl.BlockSpec(memory_space=pltpu.SMEM)] + whole(5),
        out_specs=whole(1)[0],
        compiler_params=PARAMS,
        cost_estimate=pl.CostEstimate(
            flops=2 * slots * columns * NX * count * units, bytes_accessed=5 * 2**20, transcendentals=0
        ),
    )(place, act, *blocks)


def attend(queries, keys, values, lengths):
    group_rows, ctx_len, head_size = keys.shape
    query_heads = queries.reshape(group_rows, -1, head_size)
    scores = jnp.einsum("rhd,rjd->rhj", query_heads, keys, preferred_element_type=F32)
    scores = scores * head_size ** (-0.5)
    valid = jnp.arange(ctx_len, dtype=jnp.int32)[None, None, :] < lengths[:, None, None]
    scores = jnp.where(valid, scores, -1e30)
    highest = jnp.max(scores, axis=-1, keepdims=True)
    weights = jnp.exp(scores - highest)
    probs = (weights / jnp.sum(weights, axis=-1, keepdims=True)).astype(BF16)
    attn = jnp.einsum("rhj,rjd->rhd", probs, values, preferred_element_type=F32)
    return attn.astype(BF16).reshape(queries.shape)


def shards(
    queries,
    keys,
    values,
    lengths,
    out_weight,
    residual,
    norm_gain,
    routes,
    route_weight,
    up_weight,
    down_weight,
):
    experts = lax.axis_size(("pool", "tp"))
    block_index = lax.axis_index(("pool", "tp"))
    group_index = lax.axis_index(GRP)
    x_index, member = group_index // (NZ * PAIR), group_index % PAIR
    rows, columns = residual.shape
    top_count = routes.shape[1]
    slot_cap = min(rows, rows * top_count * 2 // experts)
    slots = experts * slot_cap
    width = norm_gain.shape[0]
    units = up_weight.shape[2]
    parts = NX * PAIR

    own_routes = lax.dynamic_slice_in_dim(routes, block_index * rows, rows, 0)
    own_weight = lax.dynamic_slice_in_dim(route_weight, block_index * rows, rows, 0)
    named = own_routes.T[:, None, :] == jnp.arange(experts, dtype=jnp.int32)[None, :, None]
    weight_of = jnp.sum(jnp.where(named, own_weight.T[:, None, :], 0.0), axis=0)
    named = jnp.any(named, axis=0)
    earlier = jnp.arange(rows)[:, None] < jnp.arange(rows)[None, :]
    place = jnp.dot(named.astype(BF16), earlier.astype(BF16), preferred_element_type=F32)
    here = place.astype(jnp.int32)[:, None, :] == jnp.arange(slot_cap, dtype=jnp.int32)[None, :, None]
    here = jnp.logical_and(here, named[:, None, :])
    select = here.astype(BF16).reshape(slots, rows)
    combine = jnp.where(here, weight_of[:, None, :], 0.0).reshape(slots, rows)

    attn = attend(queries, keys, values, lengths)
    def up_cut(step):
        wanted = (x_index + step) % NX
        return lax.dynamic_slice_in_dim(up_weight[0], wanted * (width // NX), width // NX, 0)

    def down_cut(step):
        wanted = (x_index + step) % NX
        return lax.dynamic_slice_in_dim(down_weight[0], wanted * (8 * units), 8 * units, 1)

    def along(block, step):
        return lax.ppermute(block, GRP, moves(step, 0))

    attn = spread(attn, NZ, "zpair")
    attn, up1, up3 = lax.optimization_barrier((attn, up_cut(1), up_cut(3)))
    attn = spread(attn.reshape(-1, attn.shape[2]), parts, ("x", "member"))
    projected = project(attn.reshape(parts, NZ, -1, attn.shape[2]), out_weight.T)
    projected, up1, up3, up_weight, down_weight = lax.optimization_barrier(
        (projected, up1, up3, up_weight, down_weight)
    )
    projected = exchange(projected, ("pool", "tp"))
    up = [up_cut(0), along(up1, 1), up_cut(2), along(up3, 3)]
    down = [down_cut(step) for step in range(NX)]
    projected, up, down = lax.optimization_barrier((projected, up, down))
    slot_rows = head_sum(projected, residual, select)
    slot_rows, up, down = lax.optimization_barrier((slot_rows, up, down))
    same = exchange(slot_rows.reshape(NZ * experts, slot_cap, columns), ("zpair", "pool", "tp"))
    same = same.reshape(NZ, slots, columns)
    before = lax.ppermute(same[: NZ // 2], GRP, turns(1))
    after = lax.ppermute(same[NZ // 2 :], GRP, turns(-1))
    down[1], down[3], up[2] = along(down[1], 1), along(down[3], 3), along(up[2], 2)
    before, after, down[1], down[3] = lax.optimization_barrier((before, after, down[1], down[3]))
    up = [w.reshape(NZ, PAIR, columns, units) for w in up]
    gain = norm_gain.reshape(NX, NZ, PAIR, columns)
    gain = lax.dynamic_index_in_dim(gain, x_index, 0, keepdims=False)
    gain = [lax.dynamic_index_in_dim(gain, m, 1, keepdims=False) for m in (member, 1 - member)]
    gain = jnp.concatenate(gain)
    place = jnp.stack([x_index, member]).astype(jnp.int32)
    partial_up = up_product(place, (same, before, after), gain, up)
    total_up = jnp.sum(exchange(partial_up, "x").astype(F32), axis=0)
    count = slots // units
    squares = (total_up[slots : slots + count] + total_up[slots + count : slots + 2 * count]).reshape(slots, 1)
    scale = lax.rsqrt(squares / width + 1e-06)
    act = jax.nn.silu(total_up[:slots] * scale).astype(BF16)

    act, down[2] = lax.optimization_barrier((act, down[2]))
    down[2] = along(down[2], 2)
    act = spread(act, 8, ("zpair", "member"))
    partial_out = exchange(down_product(place, act, down), "x")
    expert_out = jnp.sum(partial_out.astype(F32), axis=0).astype(BF16).T
    returned = exchange(expert_out.reshape(experts, slot_cap, columns), ("pool", "tp"))
    returned = returned.reshape(slots, columns)
    high = lax.reduce_precision(combine, 8, 7)
    dims = (((0,), (0,)), ((), ()))
    result = lax.dot_general(high.astype(BF16), returned, dims, preferred_element_type=F32)
    result += lax.dot_general((combine - high).astype(BF16), returned, dims, preferred_element_type=F32)
    return result.astype(BF16)


def solution(mesh):
    devices = mesh.devices.reshape(2, NX, NZ, PAIR, 8)
    finer = Mesh(devices, ("pool",) + GRP + ("tp",), axis_types=(mesh.axis_types[0],) * 5)
    placed = (
        P(GRP, ("pool", "tp")),
        P(GRP, None, None),
        P(GRP, None, None),
        P(GRP),
        P(("pool", "tp"), GRP),
        P(("pool", "tp"), GRP),
        P(),
        P(),
        P(),
        P(("pool", "tp"), None, GRP),
        P(("pool", "tp"), GRP, None),
    )
    return jax.shard_map(
        shards, mesh=finer, in_specs=placed, out_specs=P(("pool", "tp"), GRP), check_vma=False
    )
```

```python
import jax
import jax.numpy as jnp
from jax import lax
from jax.experimental import pallas as pl
from jax.experimental.pallas import tpu as pltpu
from jax.sharding import Mesh
from jax.sharding import PartitionSpec as P

BF16 = jnp.bfloat16
F32 = jnp.float32
NX, NZ, PAIR = 4, 4, 2
GRP = ("x", "zpair", "member")


def moves(by_x, by_member):
    return [
        (x * 8 + z * 2 + m, (x + by_x) % NX * 8 + z * 2 + (m + by_member) % PAIR)
        for x in range(NX)
        for z in range(NZ)
        for m in range(PAIR)
    ]


def turns(by):
    return [(x * 8 + z, x * 8 + (z + by) % 8) for x in range(NX) for z in range(8)]


def exchange(value, axis):
    return lax.all_to_all(value, axis, 0, 0, tiled=True)


def spread(value, count, axis):
    return exchange(jnp.broadcast_to(value[None], (count,) + value.shape), axis)


def whole(count):
    return [pl.BlockSpec(memory_space=pltpu.VMEM)] * count


PARAMS = pltpu.CompilerParams(vmem_limit_bytes=40 * 2**20)


def project_kernel(attn, weight, out):
    run = attn.shape[2]
    dims = (((1,), (1,)), ((), ()))
    for x in range(NX):
        value = jnp.concatenate(
            [attn[x * PAIR + m].reshape(NZ * run, attn.shape[3]) for m in range(PAIR)], axis=0
        )
        value = lax.dot_general(value, weight[...], dims, preferred_element_type=F32).astype(BF16)
        for m in range(PAIR):
            for z in range(NZ):
                first = (m * NZ + z) * run
                out[x * NZ + z, m * run : (m + 1) * run] = value[first : first + run]


def project(attn, weight):
    rows, columns = PAIR * attn.shape[2], weight.shape[0]
    return pl.pallas_call(
        project_kernel,
        out_shape=jax.ShapeDtypeStruct((NX * NZ, rows, columns), BF16),
        in_specs=whole(2),
        out_specs=whole(1)[0],
        compiler_params=PARAMS,
        cost_estimate=pl.CostEstimate(
            flops=2 * NX * NZ * rows * columns * weight.shape[1], bytes_accessed=2 * 2**20, transcendentals=0
        ),
    )(attn, weight)


def head_sum_kernel(parts, residual, select, out):
    total = residual[...].astype(F32)
    for i in range(parts.shape[0]):
        total += parts[i].astype(F32)
    value = jnp.dot(select[...], total.astype(BF16), preferred_element_type=F32).astype(BF16)
    for z in range(NZ):
        out[z] = value


def head_sum(parts, residual, select):
    slots, columns = select.shape[0], residual.shape[1]
    return pl.pallas_call(
        head_sum_kernel,
        out_shape=jax.ShapeDtypeStruct((NZ, slots, columns), BF16),
        in_specs=whole(3),
        out_specs=whole(1)[0],
        compiler_params=PARAMS,
        cost_estimate=pl.CostEstimate(
            flops=2 * slots * columns * residual.shape[0], bytes_accessed=2**20, transcendentals=0
        ),
    )(parts, residual, select)


def up_kernel(place, same, before, after, gain, block0, block1, block2, block3, out):
    x_index, member = place[0], place[1]
    slots, units = same.shape[1], out.shape[2]
    ones = jnp.ones((16, same.shape[2]), BF16)
    dims = (((1,), (1,)), ((), ()))
    rows = [same[z] for z in range(NZ)] + [r[z] for r in (before, after) for z in range(NZ // 2)]
    normed, squares = [], 0.0
    for i, value in enumerate(rows):
        value = value.astype(F32)
        normed.append((value * gain[i : i + 1, :]).astype(BF16))
        square = value * value
        high = square.astype(BF16)
        low = (square - high.astype(F32)).astype(BF16)
        squares += lax.dot_general(ones, high, dims, preferred_element_type=F32)
        squares += lax.dot_general(ones, low, dims, preferred_element_type=F32)
    row = lax.broadcasted_iota(jnp.int32, (16, units), 0)
    count = slots // units
    tail = jnp.zeros((16, units), F32)
    for i in range(count):
        part = squares[:, i * units : (i + 1) * units]
        high = part.astype(BF16).astype(F32)
        tail = jnp.where(row == i, high, tail)
        tail = jnp.where(row == count + i, part - high, tail)
    tail = tail.astype(BF16)
    for step, block in ((0, (block0, block1)), (2, (block2, block3))):
        total = 0.0
        for i, value in enumerate(normed):
            which = member if i < NZ else 1 - member
            weight = jnp.concatenate([b[i % NZ, which] for b in block], axis=1)
            total += jnp.dot(value, weight, preferred_element_type=F32)
        total = total.astype(BF16)
        for i in range(2):
            target = lax.rem(x_index + NX - step - i, NX)
            out[target, :slots] = total[:, i * units : (i + 1) * units]
            out[target, slots:] = tail


def up_product(place, rows, gain, blocks):
    count, slots, columns = rows[0].shape
    units = blocks[0].shape[3]
    return pl.pallas_call(
        up_kernel,
        out_shape=jax.ShapeDtypeStruct((NX, slots + 16, units), BF16),
        in_specs=[pl.BlockSpec(memory_space=pltpu.SMEM)] + whole(8),
        out_specs=whole(1)[0],
        compiler_params=PARAMS,
        cost_estimate=pl.CostEstimate(
            flops=4 * slots * columns * count * NX * units, bytes_accessed=6 * 2**20, transcendentals=0
        ),
    )(place, *rows, gain, *blocks)


def down_kernel(place, act, block0, block1, block2, block3, out):
    x_index = place[0]
    count, units = act.shape[0], act.shape[2]
    dims = (((1,), (1,)), ((), ()))
    joined = [jnp.concatenate([act[z], act[z + 1]], axis=1) for z in range(0, count, 2)]
    for step, block in enumerate((block0, block1, block2, block3)):
        total = 0.0
        for z in range(count // 2):
            weight = block[:, 2 * z * units : 2 * (z + 1) * units]
            total += lax.dot_general(weight, joined[z], dims, preferred_element_type=F32)
        out[lax.rem(x_index + NX - step, NX)] = total.astype(BF16)


def down_product(place, act, blocks):
    count, slots, units = act.shape
    columns = blocks[0].shape[0]
    return pl.pallas_call(
        down_kernel,
        out_shape=jax.ShapeDtypeStruct((NX, columns, slots), BF16),
        in_specs=[pl.BlockSpec(memory_space=pltpu.SMEM)] + whole(5),
        out_specs=whole(1)[0],
        compiler_params=PARAMS,
        cost_estimate=pl.CostEstimate(
            flops=2 * slots * columns * NX * count * units, bytes_accessed=5 * 2**20, transcendentals=0
        ),
    )(place, act, *blocks)


def attend(queries, keys, values, lengths):
    group_rows, ctx_len, head_size = keys.shape
    query_heads = queries.reshape(group_rows, -1, head_size)
    scores = jnp.einsum("rhd,rjd->rhj", query_heads, keys, preferred_element_type=F32)
    scores = scores * head_size ** (-0.5)
    valid = jnp.arange(ctx_len, dtype=jnp.int32)[None, None, :] < lengths[:, None, None]
    scores = jnp.where(valid, scores, -1e30)
    highest = jnp.max(scores, axis=-1, keepdims=True)
    weights = jnp.exp(scores - highest)
    probs = (weights / jnp.sum(weights, axis=-1, keepdims=True)).astype(BF16)
    attn = jnp.einsum("rhj,rjd->rhd", probs, values, preferred_element_type=F32)
    return attn.astype(BF16).reshape(queries.shape)


def shards(
    queries,
    keys,
    values,
    lengths,
    out_weight,
    residual,
    norm_gain,
    routes,
    route_weight,
    up_weight,
    down_weight,
):
    experts = lax.axis_size(("pool", "tp"))
    block_index = lax.axis_index(("pool", "tp"))
    group_index = lax.axis_index(GRP)
    x_index, member = group_index // (NZ * PAIR), group_index % PAIR
    rows, columns = residual.shape
    top_count = routes.shape[1]
    slot_cap = min(rows, rows * top_count * 2 // experts)
    slots = experts * slot_cap
    width = norm_gain.shape[0]
    units = up_weight.shape[2]
    parts = NX * PAIR

    own_routes = lax.dynamic_slice_in_dim(routes, block_index * rows, rows, 0)
    own_weight = lax.dynamic_slice_in_dim(route_weight, block_index * rows, rows, 0)
    named = own_routes.T[:, None, :] == jnp.arange(experts, dtype=jnp.int32)[None, :, None]
    weight_of = jnp.sum(jnp.where(named, own_weight.T[:, None, :], 0.0), axis=0)
    named = jnp.any(named, axis=0)
    earlier = jnp.arange(rows)[:, None] < jnp.arange(rows)[None, :]
    place = jnp.dot(named.astype(BF16), earlier.astype(BF16), preferred_element_type=F32)
    here = place.astype(jnp.int32)[:, None, :] == jnp.arange(slot_cap, dtype=jnp.int32)[None, :, None]
    here = jnp.logical_and(here, named[:, None, :])
    select = here.astype(BF16).reshape(slots, rows)
    combine = jnp.where(here, weight_of[:, None, :], 0.0).reshape(slots, rows)

    attn = attend(queries, keys, values, lengths)
    def up_cut(step):
        wanted = (x_index + step) % NX
        return lax.dynamic_slice_in_dim(up_weight[0], wanted * (width // NX), width // NX, 0)

    def down_cut(step):
        wanted = (x_index + step) % NX
        return lax.dynamic_slice_in_dim(down_weight[0], wanted * (8 * units), 8 * units, 1)

    def along(block, step):
        return lax.ppermute(block, GRP, moves(step, 0))

    attn = spread(attn, NZ, "zpair")
    attn, up1, up3 = lax.optimization_barrier((attn, up_cut(1), up_cut(3)))
    attn = spread(attn.reshape(-1, attn.shape[2]), parts, ("x", "member"))
    projected = project(attn.reshape(parts, NZ, -1, attn.shape[2]), out_weight.T)
    projected, up1, up3, up_weight, down_weight = lax.optimization_barrier(
        (projected, up1, up3, up_weight, down_weight)
    )
    projected = exchange(projected, ("pool", "tp"))
    up = [up_cut(0), up1, up_cut(2), along(up3, 3)]
    down = [down_cut(step) for step in range(NX)]
    projected, up, down = lax.optimization_barrier((projected, up, down))
    slot_rows = head_sum(projected, residual, select)
    slot_rows, up, down = lax.optimization_barrier((slot_rows, up, down))
    same = exchange(slot_rows.reshape(NZ * experts, slot_cap, columns), ("zpair", "pool", "tp"))
    same = same.reshape(NZ, slots, columns)
    before = lax.ppermute(same[: NZ // 2], GRP, turns(1))
    after = lax.ppermute(same[NZ // 2 :], GRP, turns(-1))
    up[1], up[2], down[1], down[3] = along(up[1], 1), along(up[2], 2), along(down[1], 1), along(down[3], 3)
    before, after, down[1], down[3] = lax.optimization_barrier((before, after, down[1], down[3]))
    up = [w.reshape(NZ, PAIR, columns, units) for w in up]
    gain = norm_gain.reshape(NX, NZ, PAIR, columns)
    gain = lax.dynamic_index_in_dim(gain, x_index, 0, keepdims=False)
    gain = [lax.dynamic_index_in_dim(gain, m, 1, keepdims=False) for m in (member, 1 - member)]
    gain = jnp.concatenate(gain)
    place = jnp.stack([x_index, member]).astype(jnp.int32)
    partial_up = up_product(place, (same, before, after), gain, up)
    total_up = jnp.sum(exchange(partial_up, "x").astype(F32), axis=0)
    count = slots // units
    squares = (total_up[slots : slots + count] + total_up[slots + count : slots + 2 * count]).reshape(slots, 1)
    scale = lax.rsqrt(squares / width + 1e-06)
    act = jax.nn.silu(total_up[:slots] * scale).astype(BF16)

    act, down[2] = lax.optimization_barrier((act, down[2]))
    down[2] = along(down[2], 2)
    act = spread(act, 8, ("zpair", "member"))
    partial_out = exchange(down_product(place, act, down), "x")
    expert_out = jnp.sum(partial_out.astype(F32), axis=0).astype(BF16).T
    returned = exchange(expert_out.reshape(experts, slot_cap, columns), ("pool", "tp"))
    returned = returned.reshape(slots, columns)
    high = lax.reduce_precision(combine, 8, 7)
    dims = (((0,), (0,)), ((), ()))
    result = lax.dot_general(high.astype(BF16), returned, dims, preferred_element_type=F32)
    result += lax.dot_general((combine - high).astype(BF16), returned, dims, preferred_element_type=F32)
    return result.astype(BF16)


def solution(mesh):
    devices = mesh.devices.reshape(2, NX, NZ, PAIR, 8)
    finer = Mesh(devices, ("pool",) + GRP + ("tp",), axis_types=(mesh.axis_types[0],) * 5)
    placed = (
        P(GRP, ("pool", "tp")),
        P(GRP, None, None),
        P(GRP, None, None),
        P(GRP),
        P(("pool", "tp"), GRP),
        P(("pool", "tp"), GRP),
        P(),
        P(),
        P(),
        P(("pool", "tp"), None, GRP),
        P(("pool", "tp"), GRP, None),
    )
    return jax.shard_map(
        shards, mesh=finer, in_specs=placed, out_specs=P(("pool", "tp"), GRP), check_vma=False
    )
```

```python
import jax
import jax.numpy as jnp
from jax import lax
from jax.experimental import pallas as pl
from jax.experimental.pallas import tpu as pltpu
from jax.sharding import Mesh
from jax.sharding import PartitionSpec as P

BF16 = jnp.bfloat16
F32 = jnp.float32
NX, NZ, PAIR = 4, 4, 2
GRP = ("x", "zpair", "member")


def moves(by_x, by_member):
    return [
        (x * 8 + z * 2 + m, (x + by_x) % NX * 8 + z * 2 + (m + by_member) % PAIR)
        for x in range(NX)
        for z in range(NZ)
        for m in range(PAIR)
    ]


def turns(by):
    return [(x * 8 + z, x * 8 + (z + by) % 8) for x in range(NX) for z in range(8)]


def exchange(value, axis):
    return lax.all_to_all(value, axis, 0, 0, tiled=True)


def spread(value, count, axis):
    return exchange(jnp.broadcast_to(value[None], (count,) + value.shape), axis)


def whole(count):
    return [pl.BlockSpec(memory_space=pltpu.VMEM)] * count


PARAMS = pltpu.CompilerParams(vmem_limit_bytes=40 * 2**20)


def project_kernel(attn, weight, out):
    run = attn.shape[2]
    dims = (((1,), (1,)), ((), ()))
    for x in range(NX):
        value = jnp.concatenate(
            [attn[x * PAIR + m].reshape(NZ * run, attn.shape[3]) for m in range(PAIR)], axis=0
        )
        value = lax.dot_general(value, weight[...], dims, preferred_element_type=F32).astype(BF16)
        for m in range(PAIR):
            for z in range(NZ):
                first = (m * NZ + z) * run
                out[x * NZ + z, m * run : (m + 1) * run] = value[first : first + run]


def project(attn, weight):
    rows, columns = PAIR * attn.shape[2], weight.shape[0]
    return pl.pallas_call(
        project_kernel,
        out_shape=jax.ShapeDtypeStruct((NX * NZ, rows, columns), BF16),
        in_specs=whole(2),
        out_specs=whole(1)[0],
        compiler_params=PARAMS,
        cost_estimate=pl.CostEstimate(
            flops=2 * NX * NZ * rows * columns * weight.shape[1], bytes_accessed=2 * 2**20, transcendentals=0
        ),
    )(attn, weight)


def head_sum_kernel(parts, residual, select, out):
    total = residual[...].astype(F32)
    for i in range(parts.shape[0]):
        total += parts[i].astype(F32)
    value = jnp.dot(select[...], total.astype(BF16), preferred_element_type=F32).astype(BF16)
    for z in range(NZ):
        out[z] = value


def head_sum(parts, residual, select):
    slots, columns = select.shape[0], residual.shape[1]
    return pl.pallas_call(
        head_sum_kernel,
        out_shape=jax.ShapeDtypeStruct((NZ, slots, columns), BF16),
        in_specs=whole(3),
        out_specs=whole(1)[0],
        compiler_params=PARAMS,
        cost_estimate=pl.CostEstimate(
            flops=2 * slots * columns * residual.shape[0], bytes_accessed=2**20, transcendentals=0
        ),
    )(parts, residual, select)


def up_kernel(place, same, before, after, gain, block0, block1, block2, block3, out):
    x_index, member = place[0], place[1]
    slots, units = same.shape[1], out.shape[2]
    ones = jnp.ones((16, same.shape[2]), BF16)
    dims = (((1,), (1,)), ((), ()))
    rows = [same[z] for z in range(NZ)] + [r[z] for r in (before, after) for z in range(NZ // 2)]
    normed, squares = [], 0.0
    for i, value in enumerate(rows):
        value = value.astype(F32)
        normed.append((value * gain[i : i + 1, :]).astype(BF16))
        square = value * value
        high = square.astype(BF16)
        low = (square - high.astype(F32)).astype(BF16)
        squares += lax.dot_general(ones, high, dims, preferred_element_type=F32)
        squares += lax.dot_general(ones, low, dims, preferred_element_type=F32)
    row = lax.broadcasted_iota(jnp.int32, (16, units), 0)
    count = slots // units
    tail = jnp.zeros((16, units), F32)
    for i in range(count):
        part = squares[:, i * units : (i + 1) * units]
        high = part.astype(BF16).astype(F32)
        tail = jnp.where(row == i, high, tail)
        tail = jnp.where(row == count + i, part - high, tail)
    tail = tail.astype(BF16)
    for step, block in ((0, (block0, block1)), (2, (block2, block3))):
        total = 0.0
        for i, value in enumerate(normed):
            which = member if i < NZ else 1 - member
            weight = jnp.concatenate([b[i % NZ, which] for b in block], axis=1)
            total += jnp.dot(value, weight, preferred_element_type=F32)
        total = total.astype(BF16)
        for i in range(2):
            target = lax.rem(x_index + NX - step - i, NX)
            out[target, :slots] = total[:, i * units : (i + 1) * units]
            out[target, slots:] = tail


def up_product(place, rows, gain, blocks):
    count, slots, columns = rows[0].shape
    units = blocks[0].shape[3]
    return pl.pallas_call(
        up_kernel,
        out_shape=jax.ShapeDtypeStruct((NX, slots + 16, units), BF16),
        in_specs=[pl.BlockSpec(memory_space=pltpu.SMEM)] + whole(8),
        out_specs=whole(1)[0],
        compiler_params=PARAMS,
        cost_estimate=pl.CostEstimate(
            flops=4 * slots * columns * count * NX * units, bytes_accessed=6 * 2**20, transcendentals=0
        ),
    )(place, *rows, gain, *blocks)


def down_kernel(place, act, block0, block1, block2, block3, out):
    x_index = place[0]
    count, units = act.shape[0], act.shape[2]
    dims = (((1,), (1,)), ((), ()))
    joined = [jnp.concatenate([act[z], act[z + 1]], axis=1) for z in range(0, count, 2)]
    for step, block in enumerate((block0, block1, block2, block3)):
        total = 0.0
        for z in range(count // 2):
            weight = block[:, 2 * z * units : 2 * (z + 1) * units]
            total += lax.dot_general(weight, joined[z], dims, preferred_element_type=F32)
        out[lax.rem(x_index + NX - step, NX)] = total.astype(BF16)


def down_product(place, act, blocks):
    count, slots, units = act.shape
    columns = blocks[0].shape[0]
    return pl.pallas_call(
        down_kernel,
        out_shape=jax.ShapeDtypeStruct((NX, columns, slots), BF16),
        in_specs=[pl.BlockSpec(memory_space=pltpu.SMEM)] + whole(5),
        out_specs=whole(1)[0],
        compiler_params=PARAMS,
        cost_estimate=pl.CostEstimate(
            flops=2 * slots * columns * NX * count * units, bytes_accessed=5 * 2**20, transcendentals=0
        ),
    )(place, act, *blocks)


def attend(queries, keys, values, lengths):
    group_rows, ctx_len, head_size = keys.shape
    query_heads = queries.reshape(group_rows, -1, head_size)
    scores = jnp.einsum("rhd,rjd->rhj", query_heads, keys, preferred_element_type=F32)
    scores = scores * head_size ** (-0.5)
    valid = jnp.arange(ctx_len, dtype=jnp.int32)[None, None, :] < lengths[:, None, None]
    scores = jnp.where(valid, scores, -1e30)
    highest = jnp.max(scores, axis=-1, keepdims=True)
    weights = jnp.exp(scores - highest)
    probs = (weights / jnp.sum(weights, axis=-1, keepdims=True)).astype(BF16)
    attn = jnp.einsum("rhj,rjd->rhd", probs, values, preferred_element_type=F32)
    return attn.astype(BF16).reshape(queries.shape)


def shards(
    queries,
    keys,
    values,
    lengths,
    out_weight,
    residual,
    norm_gain,
    routes,
    route_weight,
    up_weight,
    down_weight,
):
    experts = lax.axis_size(("pool", "tp"))
    block_index = lax.axis_index(("pool", "tp"))
    group_index = lax.axis_index(GRP)
    x_index, member = group_index // (NZ * PAIR), group_index % PAIR
    rows, columns = residual.shape
    top_count = routes.shape[1]
    slot_cap = min(rows, rows * top_count * 2 // experts)
    slots = experts * slot_cap
    width = norm_gain.shape[0]
    units = up_weight.shape[2]
    parts = NX * PAIR

    own_routes = lax.dynamic_slice_in_dim(routes, block_index * rows, rows, 0)
    own_weight = lax.dynamic_slice_in_dim(route_weight, block_index * rows, rows, 0)
    named = own_routes.T[:, None, :] == jnp.arange(experts, dtype=jnp.int32)[None, :, None]
    weight_of = jnp.sum(jnp.where(named, own_weight.T[:, None, :], 0.0), axis=0)
    named = jnp.any(named, axis=0)
    earlier = jnp.arange(rows)[:, None] < jnp.arange(rows)[None, :]
    place = jnp.dot(named.astype(BF16), earlier.astype(BF16), preferred_element_type=F32)
    here = place.astype(jnp.int32)[:, None, :] == jnp.arange(slot_cap, dtype=jnp.int32)[None, :, None]
    here = jnp.logical_and(here, named[:, None, :])
    select = here.astype(BF16).reshape(slots, rows)
    combine = jnp.where(here, weight_of[:, None, :], 0.0).reshape(slots, rows)

    attn = attend(queries, keys, values, lengths)
    def up_cut(step):
        wanted = (x_index + step) % NX
        return lax.dynamic_slice_in_dim(up_weight[0], wanted * (width // NX), width // NX, 0)

    def down_cut(step):
        wanted = (x_index + step) % NX
        return lax.dynamic_slice_in_dim(down_weight[0], wanted * (8 * units), 8 * units, 1)

    def along(block, step):
        return lax.ppermute(block, GRP, moves(step, 0))

    attn = spread(attn, NZ, "zpair")
    attn, up1, up3 = lax.optimization_barrier((attn, up_cut(1), up_cut(3)))
    attn = spread(attn.reshape(-1, attn.shape[2]), parts, ("x", "member"))
    projected = project(attn.reshape(parts, NZ, -1, attn.shape[2]), out_weight.T)
    projected, up1, up3, up_weight, down_weight = lax.optimization_barrier(
        (projected, up1, up3, up_weight, down_weight)
    )
    projected = exchange(projected, ("pool", "tp"))
    up = [up_cut(0), up1, up_cut(2), up3]
    down = [down_cut(step) for step in range(NX)]
    projected, up, down = lax.optimization_barrier((projected, up, down))
    slot_rows = head_sum(projected, residual, select)
    slot_rows, up, down = lax.optimization_barrier((slot_rows, up, down))
    same = exchange(slot_rows.reshape(NZ * experts, slot_cap, columns), ("zpair", "pool", "tp"))
    same = same.reshape(NZ, slots, columns)
    before = lax.ppermute(same[: NZ // 2], GRP, turns(1))
    after = lax.ppermute(same[NZ // 2 :], GRP, turns(-1))
    up[1:] = [along(up[step], step) for step in range(1, NX)]
    down[1], down[3] = along(down[1], 1), along(down[3], 3)
    before, after, down[1], down[3] = lax.optimization_barrier((before, after, down[1], down[3]))
    up = [w.reshape(NZ, PAIR, columns, units) for w in up]
    gain = norm_gain.reshape(NX, NZ, PAIR, columns)
    gain = lax.dynamic_index_in_dim(gain, x_index, 0, keepdims=False)
    gain = [lax.dynamic_index_in_dim(gain, m, 1, keepdims=False) for m in (member, 1 - member)]
    gain = jnp.concatenate(gain)
    place = jnp.stack([x_index, member]).astype(jnp.int32)
    partial_up = up_product(place, (same, before, after), gain, up)
    total_up = jnp.sum(exchange(partial_up, "x").astype(F32), axis=0)
    count = slots // units
    squares = (total_up[slots : slots + count] + total_up[slots + count : slots + 2 * count]).reshape(slots, 1)
    scale = lax.rsqrt(squares / width + 1e-06)
    act = jax.nn.silu(total_up[:slots] * scale).astype(BF16)

    act, down[2] = lax.optimization_barrier((act, down[2]))
    down[2] = along(down[2], 2)
    act = spread(act, 8, ("zpair", "member"))
    partial_out = exchange(down_product(place, act, down), "x")
    expert_out = jnp.sum(partial_out.astype(F32), axis=0).astype(BF16).T
    returned = exchange(expert_out.reshape(experts, slot_cap, columns), ("pool", "tp"))
    returned = returned.reshape(slots, columns)
    high = lax.reduce_precision(combine, 8, 7)
    dims = (((0,), (0,)), ((), ()))
    result = lax.dot_general(high.astype(BF16), returned, dims, preferred_element_type=F32)
    result += lax.dot_general((combine - high).astype(BF16), returned, dims, preferred_element_type=F32)
    return result.astype(BF16)


def solution(mesh):
    devices = mesh.devices.reshape(2, NX, NZ, PAIR, 8)
    finer = Mesh(devices, ("pool",) + GRP + ("tp",), axis_types=(mesh.axis_types[0],) * 5)
    placed = (
        P(GRP, ("pool", "tp")),
        P(GRP, None, None),
        P(GRP, None, None),
        P(GRP),
        P(("pool", "tp"), GRP),
        P(("pool", "tp"), GRP),
        P(),
        P(),
        P(),
        P(("pool", "tp"), None, GRP),
        P(("pool", "tp"), GRP, None),
    )
    return jax.shard_map(
        shards, mesh=finer, in_specs=placed, out_specs=P(("pool", "tp"), GRP), check_vma=False
    )
```

```python
import functools

import jax
import jax.numpy as jnp
from jax import lax
from jax.experimental import pallas as pl
from jax.experimental.pallas import tpu as pltpu
from jax.sharding import Mesh
from jax.sharding import PartitionSpec as P

BF16 = jnp.bfloat16
F32 = jnp.float32
NX, NZ, PAIR = 4, 4, 2
GRP = ("x", "zpair", "member")


def moves(by_x, by_member):
    return [
        (x * 8 + z * 2 + m, (x + by_x) % NX * 8 + z * 2 + (m + by_member) % PAIR)
        for x in range(NX)
        for z in range(NZ)
        for m in range(PAIR)
    ]


def turns(by):
    return [(x * 8 + z, x * 8 + (z + by) % 8) for x in range(NX) for z in range(8)]


def exchange(value, axis):
    return lax.all_to_all(value, axis, 0, 0, tiled=True)


def spread(value, count, axis):
    return exchange(jnp.broadcast_to(value[None], (count,) + value.shape), axis)


def whole(count):
    return [pl.BlockSpec(memory_space=pltpu.VMEM)] * count


PARAMS = pltpu.CompilerParams(vmem_limit_bytes=40 * 2**20)


def project_kernel(attn, weight, out):
    run = attn.shape[2]
    dims = (((1,), (1,)), ((), ()))
    for x in range(NX):
        value = jnp.concatenate(
            [attn[x * PAIR + m].reshape(NZ * run, attn.shape[3]) for m in range(PAIR)], axis=0
        )
        value = lax.dot_general(value, weight[...], dims, preferred_element_type=F32).astype(BF16)
        for m in range(PAIR):
            for z in range(NZ):
                first = (m * NZ + z) * run
                out[x * NZ + z, m * run : (m + 1) * run] = value[first : first + run]


def project(attn, weight):
    rows, columns = PAIR * attn.shape[2], weight.shape[0]
    return pl.pallas_call(
        project_kernel,
        out_shape=jax.ShapeDtypeStruct((NX * NZ, rows, columns), BF16),
        in_specs=whole(2),
        out_specs=whole(1)[0],
        compiler_params=PARAMS,
        cost_estimate=pl.CostEstimate(
            flops=2 * NX * NZ * rows * columns * weight.shape[1], bytes_accessed=2 * 2**20, transcendentals=0
        ),
    )(attn, weight)


def head_sum_kernel(parts, residual, select, out):
    total = residual[...].astype(F32)
    for i in range(parts.shape[0]):
        total += parts[i].astype(F32)
    value = jnp.dot(select[...], total.astype(BF16), preferred_element_type=F32).astype(BF16)
    for z in range(NZ):
        out[z] = value


def head_sum(parts, residual, select):
    slots, columns = select.shape[0], residual.shape[1]
    return pl.pallas_call(
        head_sum_kernel,
        out_shape=jax.ShapeDtypeStruct((NZ, slots, columns), BF16),
        in_specs=whole(3),
        out_specs=whole(1)[0],
        compiler_params=PARAMS,
        cost_estimate=pl.CostEstimate(
            flops=2 * slots * columns * residual.shape[0], bytes_accessed=2**20, transcendentals=0
        ),
    )(parts, residual, select)


def up_kernel(place, same, before, after, gain, block0, block1, block2, block3, out):
    x_index, member = place[0], place[1]
    slots, units = same.shape[1], out.shape[2]
    ones = jnp.ones((16, same.shape[2]), BF16)
    dims = (((1,), (1,)), ((), ()))
    rows = [same[z] for z in range(NZ)] + [r[z] for r in (before, after) for z in range(NZ // 2)]
    normed, squares = [], 0.0
    for i, value in enumerate(rows):
        value = value.astype(F32)
        normed.append((value * gain[i : i + 1, :]).astype(BF16))
        square = value * value
        high = square.astype(BF16)
        low = (square - high.astype(F32)).astype(BF16)
        squares += lax.dot_general(ones, high, dims, preferred_element_type=F32)
        squares += lax.dot_general(ones, low, dims, preferred_element_type=F32)
    row = lax.broadcasted_iota(jnp.int32, (16, units), 0)
    count = slots // units
    tail = jnp.zeros((16, units), F32)
    for i in range(count):
        part = squares[:, i * units : (i + 1) * units]
        high = part.astype(BF16).astype(F32)
        tail = jnp.where(row == i, high, tail)
        tail = jnp.where(row == count + i, part - high, tail)
    tail = tail.astype(BF16)
    for step, block in ((0, (block0, block1)), (2, (block2, block3))):
        total = 0.0
        for i, value in enumerate(normed):
            which = member if i < NZ else 1 - member
            weight = jnp.concatenate([b[i % NZ, which] for b in block], axis=1)
            total += jnp.dot(value, weight, preferred_element_type=F32)
        total = total.astype(BF16)
        for i in range(2):
            target = lax.rem(x_index + NX - step - i, NX)
            out[target, :slots] = total[:, i * units : (i + 1) * units]
            out[target, slots:] = tail


def up_product(place, rows, gain, blocks):
    count, slots, columns = rows[0].shape
    units = blocks[0].shape[3]
    return pl.pallas_call(
        up_kernel,
        out_shape=jax.ShapeDtypeStruct((NX, slots + 16, units), BF16),
        in_specs=[pl.BlockSpec(memory_space=pltpu.SMEM)] + whole(8),
        out_specs=whole(1)[0],
        compiler_params=PARAMS,
        cost_estimate=pl.CostEstimate(
            flops=4 * slots * columns * count * NX * units, bytes_accessed=6 * 2**20, transcendentals=0
        ),
    )(place, *rows, gain, *blocks)


def act_kernel(parts, out, *, width):
    units = parts.shape[2]
    slots = parts.shape[1] - 16
    count = slots // units
    total = 0.0
    for i in range(parts.shape[0]):
        total += parts[i].astype(F32)
    tail = total[slots:]
    for i in range(count):
        squares = tail[i : i + 1] + tail[count + i : count + i + 1]
        scale = lax.rsqrt(jnp.broadcast_to(squares, (units, units)).T / width + 1e-06)
        value = total[i * units : (i + 1) * units] * scale
        value = (value / (1.0 + jnp.exp(-value))).astype(BF16)
        for z in range(out.shape[0]):
            out[z, i * units : (i + 1) * units] = value


def activate(parts, width):
    slots, units = parts.shape[1] - 16, parts.shape[2]
    return pl.pallas_call(
        functools.partial(act_kernel, width=width),
        out_shape=jax.ShapeDtypeStruct((8, slots, units), BF16),
        in_specs=whole(1),
        out_specs=whole(1)[0],
        compiler_params=PARAMS,
        cost_estimate=pl.CostEstimate(flops=8 * slots * units, bytes_accessed=2**20, transcendentals=slots * units),
    )(parts)


def down_kernel(place, act, block0, block1, block2, block3, out):
    x_index = place[0]
    count, units = act.shape[0], act.shape[2]
    dims = (((1,), (1,)), ((), ()))
    joined = [jnp.concatenate([act[z], act[z + 1]], axis=1) for z in range(0, count, 2)]
    for step, block in enumerate((block0, block1, block2, block3)):
        total = 0.0
        for z in range(count // 2):
            weight = block[:, 2 * z * units : 2 * (z + 1) * units]
            total += lax.dot_general(weight, joined[z], dims, preferred_element_type=F32)
        out[lax.rem(x_index + NX - step, NX)] = total.astype(BF16)


def down_product(place, act, blocks):
    count, slots, units = act.shape
    columns = blocks[0].shape[0]
    return pl.pallas_call(
        down_kernel,
        out_shape=jax.ShapeDtypeStruct((NX, columns, slots), BF16),
        in_specs=[pl.BlockSpec(memory_space=pltpu.SMEM)] + whole(5),
        out_specs=whole(1)[0],
        compiler_params=PARAMS,
        cost_estimate=pl.CostEstimate(
            flops=2 * slots * columns * NX * count * units, bytes_accessed=5 * 2**20, transcendentals=0
        ),
    )(place, act, *blocks)


def attend(queries, keys, values, lengths):
    group_rows, ctx_len, head_size = keys.shape
    query_heads = queries.reshape(group_rows, -1, head_size)
    scores = jnp.einsum("rhd,rjd->rhj", query_heads, keys, preferred_element_type=F32)
    scores = scores * head_size ** (-0.5)
    valid = jnp.arange(ctx_len, dtype=jnp.int32)[None, None, :] < lengths[:, None, None]
    scores = jnp.where(valid, scores, -1e30)
    highest = jnp.max(scores, axis=-1, keepdims=True)
    weights = jnp.exp(scores - highest)
    probs = (weights / jnp.sum(weights, axis=-1, keepdims=True)).astype(BF16)
    attn = jnp.einsum("rhj,rjd->rhd", probs, values, preferred_element_type=F32)
    return attn.astype(BF16).reshape(queries.shape)


def shards(
    queries,
    keys,
    values,
    lengths,
    out_weight,
    residual,
    norm_gain,
    routes,
    route_weight,
    up_weight,
    down_weight,
):
    experts = lax.axis_size(("pool", "tp"))
    block_index = lax.axis_index(("pool", "tp"))
    group_index = lax.axis_index(GRP)
    x_index, member = group_index // (NZ * PAIR), group_index % PAIR
    rows, columns = residual.shape
    top_count = routes.shape[1]
    slot_cap = min(rows, rows * top_count * 2 // experts)
    slots = experts * slot_cap
    width = norm_gain.shape[0]
    units = up_weight.shape[2]
    parts = NX * PAIR

    own_routes = lax.dynamic_slice_in_dim(routes, block_index * rows, rows, 0)
    own_weight = lax.dynamic_slice_in_dim(route_weight, block_index * rows, rows, 0)
    named = own_routes.T[:, None, :] == jnp.arange(experts, dtype=jnp.int32)[None, :, None]
    weight_of = jnp.sum(jnp.where(named, own_weight.T[:, None, :], 0.0), axis=0)
    named = jnp.any(named, axis=0)
    earlier = jnp.arange(rows)[:, None] < jnp.arange(rows)[None, :]
    place = jnp.dot(named.astype(BF16), earlier.astype(BF16), preferred_element_type=F32)
    here = place.astype(jnp.int32)[:, None, :] == jnp.arange(slot_cap, dtype=jnp.int32)[None, :, None]
    here = jnp.logical_and(here, named[:, None, :])
    select = here.astype(BF16).reshape(slots, rows)
    combine = jnp.where(here, weight_of[:, None, :], 0.0).reshape(slots, rows)

    attn = attend(queries, keys, values, lengths)
    def up_cut(step):
        wanted = (x_index + step) % NX
        return lax.dynamic_slice_in_dim(up_weight[0], wanted * (width // NX), width // NX, 0)

    def down_cut(step):
        wanted = (x_index + step) % NX
        return lax.dynamic_slice_in_dim(down_weight[0], wanted * (8 * units), 8 * units, 1)

    def along(block, step):
        return lax.ppermute(block, GRP, moves(step, 0))

    attn = spread(attn, NZ, "zpair")
    attn, up1, up3 = lax.optimization_barrier((attn, up_cut(1), up_cut(3)))
    attn = spread(attn.reshape(-1, attn.shape[2]), parts, ("x", "member"))
    projected = project(attn.reshape(parts, NZ, -1, attn.shape[2]), out_weight.T)
    projected, up1, up3, up_weight, down_weight = lax.optimization_barrier(
        (projected, up1, up3, up_weight, down_weight)
    )
    projected = exchange(projected, ("pool", "tp"))
    up = [up_cut(0), up1, up_cut(2), up3]
    down = [down_cut(step) for step in range(NX)]
    projected, up, down = lax.optimization_barrier((projected, up, down))
    slot_rows = head_sum(projected, residual, select)
    slot_rows, up, down = lax.optimization_barrier((slot_rows, up, down))
    same = exchange(slot_rows.reshape(NZ * experts, slot_cap, columns), ("zpair", "pool", "tp"))
    same = same.reshape(NZ, slots, columns)
    before = lax.ppermute(same[: NZ // 2], GRP, turns(1))
    after = lax.ppermute(same[NZ // 2 :], GRP, turns(-1))
    up[1:] = [along(up[step], step) for step in range(1, NX)]
    down[1], down[3] = along(down[1], 1), along(down[3], 3)
    before, after, down[1], down[3] = lax.optimization_barrier((before, after, down[1], down[3]))
    up = [w.reshape(NZ, PAIR, columns, units) for w in up]
    gain = norm_gain.reshape(NX, NZ, PAIR, columns)
    gain = lax.dynamic_index_in_dim(gain, x_index, 0, keepdims=False)
    gain = [lax.dynamic_index_in_dim(gain, m, 1, keepdims=False) for m in (member, 1 - member)]
    gain = jnp.concatenate(gain)
    place = jnp.stack([x_index, member]).astype(jnp.int32)
    partial_up = up_product(place, (same, before, after), gain, up)
    act = activate(exchange(partial_up, "x"), width)
    act, down[2] = lax.optimization_barrier((act, down[2]))
    down[2] = along(down[2], 2)
    act = exchange(act, ("zpair", "member"))
    partial_out = exchange(down_product(place, act, down), "x")
    expert_out = jnp.sum(partial_out.astype(F32), axis=0).astype(BF16).T
    returned = exchange(expert_out.reshape(experts, slot_cap, columns), ("pool", "tp"))
    returned = returned.reshape(slots, columns)
    high = lax.reduce_precision(combine, 8, 7)
    dims = (((0,), (0,)), ((), ()))
    result = lax.dot_general(high.astype(BF16), returned, dims, preferred_element_type=F32)
    result += lax.dot_general((combine - high).astype(BF16), returned, dims, preferred_element_type=F32)
    return result.astype(BF16)


def solution(mesh):
    devices = mesh.devices.reshape(2, NX, NZ, PAIR, 8)
    finer = Mesh(devices, ("pool",) + GRP + ("tp",), axis_types=(mesh.axis_types[0],) * 5)
    placed = (
        P(GRP, ("pool", "tp")),
        P(GRP, None, None),
        P(GRP, None, None),
        P(GRP),
        P(("pool", "tp"), GRP),
        P(("pool", "tp"), GRP),
        P(),
        P(),
        P(),
        P(("pool", "tp"), None, GRP),
        P(("pool", "tp"), GRP, None),
    )
    return jax.shard_map(
        shards, mesh=finer, in_specs=placed, out_specs=P(("pool", "tp"), GRP), check_vma=False
    )
```
